32 devices in a mesh: seq: 8 (over z, x), dp: 4 (over y, core).
Axes of the slice: x: 2, y: 2, z: 4, core: 2. Of those that a mesh axis runs over, the one named last changes fastest.
Arguments:
- queries: bfloat16 [4, 2048, 1024], P('dp', 'seq'), may hold values from -8 to 8
- key_rows: bfloat16 [4, 2048, 1024], P('dp', 'seq'), may hold values from -8 to 8
- value_rows: bfloat16 [4, 2048, 1024], P('dp', 'seq'), may hold values from -16 to 16
- conv_key: float32 [3, 4, 1024], replicated, may hold values from -2.5 to 2.5
- conv_value: float32 [3, 4, 1024], replicated, may hold values from -2.5 to 2.5
- grad_out: bfloat16 [4, 2048, 1024], P('dp', 'seq'), may hold values from -12 to 12
Outputs:
- attended: bfloat16 [4, 2048, 1024], P('dp', 'seq')
- grad_query: bfloat16 [4, 2048, 1024], P('dp', 'seq')
- grad_key: bfloat16 [4, 2048, 1024], P('dp', 'seq')
- grad_value: bfloat16 [4, 2048, 1024], P('dp', 'seq')
- grad_conv_key: float32 [3, 4, 1024], replicated
- grad_conv_value: float32 [3, 4, 1024], replicated
The draws below stay inside these ranges and needn't reach their ends.
All inputs are finite; a program needn't handle non-finite values.
Results may differ from the reference program's by a relative error of at most 0.019.
Values may be sent and summed in bfloat16 or wider, within the bound.
A program may use at most 128 MiB of HBM per device.

```python
import jax
import jax.numpy as jnp
from jax import lax

HEADS = 8
HEAD_DIM = 128
BLOCK = 128
D = 1024
LEVELS = 3
SEQLEN = 2048
BATCH = 4


def draw_queries(key, part):
    base_key = jax.random.fold_in(key, 11)
    drawn = jnp.clip(1.5 * jax.random.normal(base_key, (BATCH, SEQLEN, D), jnp.float32), -7.5, 7.5)
    return drawn.astype(jnp.bfloat16)


def draw_key_rows(key, part):
    base_key = jax.random.fold_in(key, 13)
    drawn = jnp.clip(jax.random.normal(base_key, (BATCH, SEQLEN, D), jnp.float32), -6.0, 6.0)
    return drawn.astype(jnp.bfloat16)


def levels(rng, extent, shards, least, high):
    def one(dim, parts):
        heights = jax.random.uniform(jax.random.fold_in(jax.random.fold_in(rng, 6), dim), (parts,), jnp.float32, least / len(shards), high / len(shards))
        return jnp.repeat(jnp.exp(heights), extent[dim] // parts).reshape((-1,) + (1,) * (len(extent) - dim - 1))

    loudness = one(*shards[0])
    for cut in shards[1:]:
        loudness = loudness * one(*cut)
    return loudness


def gaussian(rng, dims, scale, limit, split=(), held_as=jnp.bfloat16):
    values = jax.random.normal(rng, dims, jnp.float32) * scale
    if len(split) > 0:
        values = levels(rng, dims, split, -0.22, 0.18) * values
    return jnp.clip(values, min=-limit, max=limit).astype(held_as)


def setup_inputs(seed: int = 0) -> dict:
    streams_of = jax.random.split(jax.random.key(seed), 7)
    queries = draw_queries(jax.random.fold_in(streams_of[6], 71), 0)
    key_rows = draw_key_rows(jax.random.fold_in(streams_of[6], 71), 0)
    value_rows = gaussian(streams_of[2], (BATCH, SEQLEN, D), 4.0, 16.0, ((0, 4), (1, 8)))
    conv_key = gaussian(streams_of[3], (LEVELS, 4, D), 0.5, 2.5, (), jnp.float32)
    conv_value = gaussian(streams_of[4], (LEVELS, 4, D), 0.5, 2.5, (), jnp.float32)
    grad_out = gaussian(streams_of[5], (BATCH, SEQLEN, D), 2.0, 12.0, ((0, 4), (1, 8)))
    return dict(queries=queries, key_rows=key_rows, value_rows=value_rows, conv_key=conv_key, conv_value=conv_value, grad_out=grad_out)


def coarsen(extended, weight):
    out_rows = (extended.shape[0] - 2) // 2
    summed = weight[0] * extended[0:2 * out_rows:2].astype(jnp.float32)
    for offset in range(1, 4):
        summed = summed + weight[offset] * extended[offset:offset + 2 * out_rows:2].astype(jnp.float32)
    return summed.astype(jnp.bfloat16)


def coarsen_back(upstream, extended, weight):
    out_rows, feat_width = upstream.shape
    zero_row = jnp.zeros((1, feat_width), jnp.float32)
    even_rows = jnp.concatenate([weight[0] * upstream, zero_row], 0) + jnp.concatenate([zero_row, weight[2] * upstream], 0)
    odd_rows = jnp.concatenate([weight[1] * upstream, zero_row], 0) + jnp.concatenate([zero_row, weight[3] * upstream], 0)
    spread = jnp.stack([even_rows, odd_rows], 1).reshape(2 * out_rows + 2, feat_width)
    weight_grad = jnp.stack([jnp.sum(upstream * extended[offset:offset + 2 * out_rows:2].astype(jnp.float32), 0) for offset in range(4)])
    return spread, weight_grad


def one_sequence(queries, key_rows, value_rows, grad_out, conv_key, conv_value):
    seq_rows, feat_width = queries.shape
    fine_blocks = seq_rows // BLOCK
    score_scale = HEAD_DIM ** -0.5
    zero_pair = jnp.zeros((2, feat_width), jnp.bfloat16)
    pad_rows = jnp.zeros((BLOCK, feat_width), jnp.bfloat16)
    key_levels = [key_rows]
    value_levels = [value_rows]
    for level_id in range(LEVELS):
        key_levels.append(coarsen(jnp.concatenate([zero_pair, key_levels[-1]], 0), conv_key[level_id]))
        value_levels.append(coarsen(jnp.concatenate([zero_pair, value_levels[-1]], 0), conv_value[level_id]))
    key_padded = [jnp.concatenate([pad_rows, level_rows, pad_rows], 0) for level_rows in key_levels]
    value_padded = [jnp.concatenate([pad_rows, level_rows, pad_rows], 0) for level_rows in value_levels]
    key_count = (3 + 2 * LEVELS) * BLOCK

    def step(scan_state, block_id):
        key_grads, value_grads = scan_state
        key_spans = [(0, (block_id * BLOCK).astype(jnp.int32), 3 * BLOCK)]
        key_masks = [jnp.full((BLOCK,), block_id >= 1), jnp.ones((BLOCK,), jnp.bool_), jnp.full((BLOCK,), block_id + 1 < fine_blocks)]
        for level_id in range(1, LEVELS + 1):
            coarse_id = block_id // (2 ** level_id)
            key_spans.append((level_id, (coarse_id * BLOCK).astype(jnp.int32), BLOCK))
            key_masks.append(jnp.full((BLOCK,), coarse_id >= 1))
            key_spans.append((level_id, ((coarse_id + 2) * BLOCK).astype(jnp.int32), BLOCK))
            key_masks.append(jnp.full((BLOCK,), coarse_id + 1 < fine_blocks // (2 ** level_id)))
        key_set = jnp.concatenate([lax.dynamic_slice_in_dim(key_padded[level_id], start_row, span_rows, 0) for level_id, start_row, span_rows in key_spans], 0)
        value_set = jnp.concatenate([lax.dynamic_slice_in_dim(value_padded[level_id], start_row, span_rows, 0) for level_id, start_row, span_rows in key_spans], 0)
        valid_mask = jnp.concatenate(key_masks, 0)
        key_set = key_set.astype(jnp.float32).reshape(key_count, HEADS, HEAD_DIM)
        value_set = value_set.astype(jnp.float32).reshape(key_count, HEADS, HEAD_DIM)
        start_fine = (block_id * BLOCK).astype(jnp.int32)
        query_block = lax.dynamic_slice_in_dim(queries, start_fine, BLOCK, 0).astype(jnp.float32).reshape(BLOCK, HEADS, HEAD_DIM)
        out_block = lax.dynamic_slice_in_dim(grad_out, start_fine, BLOCK, 0).astype(jnp.float32).reshape(BLOCK, HEADS, HEAD_DIM)
        raw_scores = jnp.einsum('qhe,khe->hqk', query_block, key_set, precision=lax.Precision.HIGHEST) * score_scale
        raw_scores = jnp.where(valid_mask[None, None, :], raw_scores, -jnp.inf)
        row_max = jnp.max(raw_scores, -1, keepdims=True)
        exp_scores = jnp.exp(raw_scores - row_max)
        prob_full = exp_scores / jnp.sum(exp_scores, -1, keepdims=True)
        probs_low = prob_full.astype(jnp.bfloat16).astype(jnp.float32)
        attended = jnp.einsum('hqk,khe->qhe', probs_low, value_set, precision=lax.Precision.HIGHEST).reshape(BLOCK, feat_width).astype(jnp.bfloat16)
        grad_prob = jnp.einsum('qhe,khe->hqk', out_block, value_set, precision=lax.Precision.HIGHEST)
        row_delta = jnp.sum(prob_full * grad_prob, -1, keepdims=True)
        dscore = (prob_full * (grad_prob - row_delta) * score_scale).astype(jnp.bfloat16).astype(jnp.float32)
        grad_q = jnp.einsum('hqk,khe->qhe', dscore, key_set, precision=lax.Precision.HIGHEST).reshape(BLOCK, feat_width).astype(jnp.bfloat16)
        key_part = jnp.einsum('hqk,qhe->khe', dscore, query_block, precision=lax.Precision.HIGHEST).reshape(key_count, feat_width)
        value_part = jnp.einsum('hqk,qhe->khe', probs_low, out_block, precision=lax.Precision.HIGHEST).reshape(key_count, feat_width)
        key_grads = list(key_grads)
        value_grads = list(value_grads)
        offset = 0
        for level_id, start_row, span_rows in key_spans:
            current = lax.dynamic_slice_in_dim(key_grads[level_id], start_row, span_rows, 0)
            key_grads[level_id] = lax.dynamic_update_slice_in_dim(key_grads[level_id], current + key_part[offset:offset + span_rows], start_row, 0)
            current = lax.dynamic_slice_in_dim(value_grads[level_id], start_row, span_rows, 0)
            value_grads[level_id] = lax.dynamic_update_slice_in_dim(value_grads[level_id], current + value_part[offset:offset + span_rows], start_row, 0)
            offset += span_rows
        return (tuple(key_grads), tuple(value_grads)), (attended, grad_q)

    start_state = (tuple(jnp.zeros(level_rows.shape, jnp.float32) for level_rows in key_padded), tuple(jnp.zeros(level_rows.shape, jnp.float32) for level_rows in value_padded))
    final_state, outputs = lax.scan(step, start_state, jnp.arange(fine_blocks, dtype=jnp.int32))
    key_grads, value_grads = final_state
    attended_all = outputs[0].reshape(seq_rows, feat_width)
    grad_q_all = outputs[1].reshape(seq_rows, feat_width)
    key_flow = key_grads[LEVELS][BLOCK:-BLOCK]
    value_flow = value_grads[LEVELS][BLOCK:-BLOCK]
    key_weight_grads = [None] * LEVELS
    value_weight_grads = [None] * LEVELS
    for level_id in range(LEVELS, 0, -1):
        spread, key_weight_grads[level_id - 1] = coarsen_back(key_flow, jnp.concatenate([zero_pair, key_levels[level_id - 1]], 0), conv_key[level_id - 1])
        key_flow = key_grads[level_id - 1][BLOCK:-BLOCK] + spread[2:]
        spread, value_weight_grads[level_id - 1] = coarsen_back(value_flow, jnp.concatenate([zero_pair, value_levels[level_id - 1]], 0), conv_value[level_id - 1])
        value_flow = value_grads[level_id - 1][BLOCK:-BLOCK] + spread[2:]
    return attended_all, grad_q_all, key_flow.astype(jnp.bfloat16), value_flow.astype(jnp.bfloat16), jnp.stack(key_weight_grads), jnp.stack(value_weight_grads)


def reference(queries, key_rows, value_rows, conv_key, conv_value, grad_out):
    def per_sequence(seq_items):
        return one_sequence(seq_items[0], seq_items[1], seq_items[2], seq_items[3], conv_key, conv_value)

    results = lax.map(per_sequence, (queries, key_rows, value_rows, grad_out))
    return results[0], results[1], results[2], results[3], jnp.sum(results[4], 0), jnp.sum(results[5], 0)
```

```python
import functools

import jax
import jax.numpy as jnp
from jax import lax
from jax.experimental import pallas as pl
from jax.experimental.pallas import tpu as pltpu
from jax.sharding import PartitionSpec as P

HEADS = 8
HEAD_DIM = 128
BLOCK = 128


def passed_along(value, axis, steps):
    count = lax.axis_size(axis)
    initial, last = (max(0, -steps), min(count, count - steps))
    return lax.ppermute(value, axis, [(source, source + steps) for source in range(initial, last)])


def partner_2(array, axis, distance):
    return lax.ppermute(array, axis, [(i, i ^ 1 << distance) for i in range(lax.axis_size(axis))])


def coarsen(extended, weight):
    out_rows = (extended.shape[1] - 2) // 2
    summed = weight[0] * extended[:, 0 : 2 * out_rows : 2].astype(jnp.float32)
    for offset in range(1, 4):
        summed = summed + weight[offset] * extended[:, offset : offset + 2 * out_rows : 2].astype(
            jnp.float32
        )
    return summed.astype(jnp.bfloat16)


def coarsen_back(upstream, extended, weight):
    seqs_dev, out_rows, feat_width = upstream.shape
    zero_row = jnp.zeros((seqs_dev, 1, feat_width), jnp.float32)
    even_rows = jnp.concatenate([weight[0] * upstream, zero_row], 1) + jnp.concatenate(
        [zero_row, weight[2] * upstream], 1
    )
    odd_rows = jnp.concatenate([weight[1] * upstream, zero_row], 1) + jnp.concatenate(
        [zero_row, weight[3] * upstream], 1
    )
    spread = jnp.stack([even_rows, odd_rows], 2).reshape(seqs_dev, 2 * out_rows + 2, feat_width)
    weight_grad = jnp.stack(
        [
            jnp.sum(
                upstream * extended[:, offset : offset + 2 * out_rows : 2].astype(jnp.float32),
                (0, 1),
            )
            for offset in range(4)
        ]
    )
    return (spread, weight_grad)


def move_near(moved_rows, shift_by):
    return passed_along(moved_rows, "seq", shift_by)


def move_grads(moved_rows, shift_by):
    return passed_along(moved_rows.astype(jnp.bfloat16), "seq", shift_by).astype(moved_rows.dtype)


def per_device(queries, key_rows, value_rows, conv_key, conv_value, grad_out):
    seqs_dev, tok_rows, feat_width = queries.shape
    levels = conv_key.shape[0]
    head_count = HEADS
    head_size = HEAD_DIM
    blk_rows = BLOCK
    blocks_here = tok_rows // blk_rows
    local_top = blocks_here.bit_length() - 1
    seq_devices = lax.axis_size("seq")
    dev_index = lax.axis_index("seq")
    total_blocks = blocks_here * seq_devices
    score_scale = head_size ** (-0.5)
    pair_width = 2 * feat_width
    group_heads = 2
    kv_weight = jnp.stack(
        [
            conv_key.reshape(levels, 4, head_count, head_size),
            conv_value.reshape(levels, 4, head_count, head_size),
        ],
        3,
    ).reshape(levels, 4, pair_width)
    fine_pairs = jnp.stack(
        [
            key_rows.reshape(seqs_dev, tok_rows, head_count, head_size),
            value_rows.reshape(seqs_dev, tok_rows, head_count, head_size),
        ],
        3,
    ).reshape(seqs_dev, tok_rows, pair_width)
    own_rows = [fine_pairs]
    left_rims = [move_near(fine_pairs[:, -blk_rows:], 1)]
    right_rims = [move_near(fine_pairs[:, :blk_rows], -1)]
    extended_local = [None]
    level_id = 1
    extended = jnp.concatenate([left_rims[level_id - 1][:, -2:], own_rows[level_id - 1]], 1)
    extended_local.append(extended)
    coarse = coarsen(extended, kv_weight[level_id - 1])
    own_rows.append(coarse)
    left_rims.append(move_near(coarse, 1))
    right_rims.append(move_near(coarse, -1))
    block_now = own_rows[local_top]
    left_now = left_rims[local_top]
    group_lefts, group_rights, group_extended, group_first = ([], [], [], [])
    for level_id in range(local_top + 1, levels + 1):
        swap_bit = level_id - local_top - 1
        extended = jnp.concatenate([left_now[:, -2:], block_now], 1)
        group_extended.append(extended)
        own_half = coarsen(extended, kv_weight[level_id - 1])
        partner = partner_2(own_half, "seq", swap_bit)
        is_first = dev_index // 2**swap_bit % 2 == 0
        group_first.append(is_first)
        block_now = jnp.where(
            is_first,
            jnp.concatenate([own_half, partner], 1),
            jnp.concatenate([partner, own_half], 1),
        )
        stride_dev = 2 ** (level_id - local_top)
        left_now = move_near(block_now, stride_dev)
        right_now = move_near(block_now, -stride_dev)
        group_lefts.append(left_now)
        group_rights.append(right_now)
    glob_blocks = dev_index * blocks_here + jnp.arange(blocks_here, dtype=jnp.int32)
    always = jnp.ones((blocks_here,), jnp.bool_)
    sources = []
    pieces = []
    for level_id in range(local_top + 1):
        block_count = blocks_here >> level_id
        padded = jnp.concatenate([left_rims[level_id], own_rows[level_id], right_rims[level_id]], 1)
        sources.append(
            padded.reshape(seqs_dev, block_count + 2, blk_rows, head_count, 2, head_size)
        )
        coarse_id = glob_blocks // 2**level_id
        spread = 2**level_id
        pieces.append((level_id, 0, spread, coarse_id >= 1))
        if level_id == 0:
            pieces.append((0, 1, 1, always))
        pieces.append((level_id, 2, spread, coarse_id + 1 < total_blocks // 2**level_id))
    for slot_id in range(levels - local_top):
        level_id = local_top + 1 + slot_id
        coarse_id = glob_blocks // 2**level_id
        sources.append(
            group_lefts[slot_id].reshape(seqs_dev, 1, blk_rows, head_count, 2, head_size)
        )
        pieces.append((len(sources) - 1, 0, blocks_here, coarse_id >= 1))
        sources.append(
            group_rights[slot_id].reshape(seqs_dev, 1, blk_rows, head_count, 2, head_size)
        )
        pieces.append(
            (len(sources) - 1, 0, blocks_here, coarse_id + 1 < total_blocks // 2**level_id)
        )
    query_blocks = queries.reshape(seqs_dev, blocks_here, blk_rows, head_count, head_size)
    out_blocks = grad_out.reshape(seqs_dev, blocks_here, blk_rows, head_count, head_size)

    def head_group(group_id, loop_state):
        attended_acc, grad_q_acc, source_grads, log_totals, row_deltas = loop_state
        head_start = group_id * group_heads
        q_part = lax.dynamic_slice_in_dim(query_blocks, head_start, group_heads, 3)
        do_part = lax.dynamic_slice_in_dim(out_blocks, head_start, group_heads, 3)
        source_parts = [
            lax.dynamic_slice_in_dim(source, head_start, group_heads, 3) for source in sources
        ]
        score_list = []
        views = []
        for source_id, offset, spread, valid_mask in pieces:
            block_count = blocks_here // spread
            key_blocks = source_parts[source_id][:, offset : offset + block_count]
            q_view = q_part.reshape(seqs_dev, block_count, spread, blk_rows, group_heads, head_size)
            do_view = do_part.reshape(
                seqs_dev, block_count, spread, blk_rows, group_heads, head_size
            )
            raw_scores = jnp.einsum(
                "bnrqhe,bnkhe->bnrhqk",
                q_view,
                key_blocks[..., 0, :],
                preferred_element_type=jnp.float32,
            )
            raw_scores = (
                raw_scores.reshape(seqs_dev, blocks_here, group_heads, blk_rows, blk_rows)
                * score_scale
            )
            score_list.append(
                jnp.where(valid_mask[None, :, None, None, None], raw_scores, -jnp.inf)
            )
            views.append((key_blocks, q_view, do_view, block_count, spread))
        all_scores = jnp.concatenate(score_list, 4)
        row_max = jnp.max(all_scores, 4, keepdims=True)
        exp_scores = jnp.exp(all_scores - row_max)
        summed = jnp.sum(exp_scores, 4, keepdims=True)
        prob_full = exp_scores / summed
        probs_low = prob_full.astype(jnp.bfloat16)
        attended_part = jnp.zeros(
            (seqs_dev, blocks_here, blk_rows, group_heads, head_size), jnp.float32
        )
        grad_prob_list = []
        for piece_id, (key_blocks, q_view, do_view, block_count, spread) in enumerate(views):
            p_slice = probs_low[..., piece_id * blk_rows : (piece_id + 1) * blk_rows].reshape(
                seqs_dev, block_count, spread, group_heads, blk_rows, blk_rows
            )
            attended_part = attended_part + jnp.einsum(
                "bnrhqk,bnkhe->bnrqhe",
                p_slice,
                key_blocks[..., 1, :],
                preferred_element_type=jnp.float32,
            ).reshape(attended_part.shape)
            grad_prob = jnp.einsum(
                "bnrqhe,bnkhe->bnrhqk",
                do_view,
                key_blocks[..., 1, :],
                preferred_element_type=jnp.float32,
            )
            grad_prob_list.append(
                grad_prob.reshape(seqs_dev, blocks_here, group_heads, blk_rows, blk_rows)
            )
        grad_prob_all = jnp.concatenate(grad_prob_list, 4)
        row_delta = jnp.sum(prob_full * grad_prob_all, 4, keepdims=True)
        dscore = (prob_full * (grad_prob_all - row_delta) * score_scale).astype(jnp.bfloat16)
        grad_q_part = jnp.zeros(
            (seqs_dev, blocks_here, blk_rows, group_heads, head_size), jnp.float32
        )
        group_grads = [jnp.zeros(part_arr.shape, jnp.float32) for part_arr in source_parts]
        for piece_id, (key_blocks, q_view, do_view, block_count, spread) in enumerate(views):
            source_id, offset = (pieces[piece_id][0], pieces[piece_id][1])
            p_slice = probs_low[..., piece_id * blk_rows : (piece_id + 1) * blk_rows].reshape(
                seqs_dev, block_count, spread, group_heads, blk_rows, blk_rows
            )
            ds_slice = dscore[..., piece_id * blk_rows : (piece_id + 1) * blk_rows].reshape(
                seqs_dev, block_count, spread, group_heads, blk_rows, blk_rows
            )
            grad_q_part = grad_q_part + jnp.einsum(
                "bnrhqk,bnkhe->bnrqhe",
                ds_slice,
                key_blocks[..., 0, :],
                preferred_element_type=jnp.float32,
            ).reshape(grad_q_part.shape)
            key_grad = jnp.einsum(
                "bnrhqk,bnrqhe->bnkhe", ds_slice, q_view, preferred_element_type=jnp.float32
            )
            value_grad = jnp.einsum(
                "bnrhqk,bnrqhe->bnkhe", p_slice, do_view, preferred_element_type=jnp.float32
            )
            pair_grad = jnp.stack([key_grad, value_grad], 4)
            group_grads[source_id] = (
                group_grads[source_id].at[:, offset : offset + block_count].add(pair_grad)
            )
        attended_acc = lax.dynamic_update_slice_in_dim(
            attended_acc, attended_part.astype(jnp.bfloat16), head_start, 3
        )
        grad_q_acc = lax.dynamic_update_slice_in_dim(
            grad_q_acc, grad_q_part.astype(jnp.bfloat16), head_start, 3
        )
        source_grads = tuple(
            (
                lax.dynamic_update_slice_in_dim(whole, group_part, head_start, 3)
                for whole, group_part in zip(source_grads, group_grads)
            )
        )
        log_totals = lax.dynamic_update_slice_in_dim(
            log_totals, (row_max + jnp.log(summed))[..., 0], head_start, 2
        )
        row_deltas = lax.dynamic_update_slice_in_dim(row_deltas, row_delta[..., 0], head_start, 2)
        return (attended_acc, grad_q_acc, source_grads, log_totals, row_deltas)

    start_state = (
        jnp.zeros((seqs_dev, blocks_here, blk_rows, head_count, head_size), jnp.bfloat16),
        jnp.zeros((seqs_dev, blocks_here, blk_rows, head_count, head_size), jnp.bfloat16),
        tuple((jnp.zeros(source.shape, jnp.float32) for source in sources)),
        jnp.zeros((seqs_dev, blocks_here, head_count, blk_rows), jnp.float32),
        jnp.zeros((seqs_dev, blocks_here, head_count, blk_rows), jnp.float32),
    )
    attended_acc, grad_q_acc, source_grads, log_totals, row_deltas = lax.fori_loop(
        0, head_count // group_heads, head_group, start_state
    )
    attended = attended_acc.reshape(seqs_dev, tok_rows, feat_width)
    grad_query = grad_q_acc.reshape(seqs_dev, tok_rows, feat_width)
    grad_left, grad_own, grad_right = ([], [], [])
    for level_id in range(local_top + 1):
        flat_grad = source_grads[level_id].reshape(seqs_dev, -1, pair_width)
        grad_left.append(flat_grad[:, :blk_rows])
        grad_own.append(flat_grad[:, blk_rows:-blk_rows])
        grad_right.append(flat_grad[:, -blk_rows:])
    group_left_grads = [
        source_grads[local_top + 1 + 2 * slot_id].reshape(seqs_dev, blk_rows, pair_width)
        for slot_id in range(levels - local_top)
    ]
    group_right_grads = [
        source_grads[local_top + 2 + 2 * slot_id].reshape(seqs_dev, blk_rows, pair_width)
        for slot_id in range(levels - local_top)
    ]
    weight_grads = [None] * levels
    carry_block = jnp.zeros((seqs_dev, blk_rows, pair_width), jnp.float32)
    carry_left = jnp.zeros((seqs_dev, 2, pair_width), jnp.float32)
    for level_id in range(levels, local_top, -1):
        slot_id = level_id - local_top - 1
        stride_dev = 2 ** (level_id - local_top)
        left_total = group_left_grads[slot_id].at[:, -2:].add(carry_left)
        block_total = (
            carry_block
            + move_grads(left_total, -stride_dev)
            + move_grads(group_right_grads[slot_id], stride_dev)
        )
        first_part = block_total[:, : blk_rows // 2]
        second_part = block_total[:, blk_rows // 2 :]
        keep_part = jnp.where(group_first[slot_id], first_part, second_part)
        give_part = jnp.where(group_first[slot_id], second_part, first_part)
        half_grad = keep_part + partner_2(give_part.astype(jnp.bfloat16), "seq", slot_id).astype(
            give_part.dtype
        )
        spread, weight_grads[level_id - 1] = coarsen_back(
            half_grad, group_extended[slot_id], kv_weight[level_id - 1]
        )
        carry_left = spread[:, :2]
        carry_block = spread[:, 2:]
    grad_left[local_top] = grad_left[local_top].at[:, -2:].add(carry_left)
    grad_own[local_top] = grad_own[local_top] + carry_block
    fine_left_conv = jnp.zeros((seqs_dev, blk_rows, pair_width), jnp.float32)
    level_id = 1
    from_right = move_grads(grad_left[level_id], -1)
    from_left = move_grads(grad_right[level_id], 1)
    level_grad = (
        grad_own[level_id].at[:, :blk_rows].add(from_left).at[:, -blk_rows:].add(from_right)
    )
    spread, weight_grads[level_id - 1] = coarsen_back(
        level_grad, extended_local[level_id], kv_weight[level_id - 1]
    )
    fine_left_conv = fine_left_conv.at[:, -2:].add(spread[:, :2])
    grad_own[level_id - 1] = grad_own[level_id - 1] + spread[:, 2:]

    def owner_terms(sent_rows, sent_stats, pair_rows):
        q_rows = sent_rows[:, :, :feat_width].reshape(seqs_dev, blk_rows, head_count, head_size)
        do_rows = sent_rows[:, :, feat_width:].reshape(seqs_dev, blk_rows, head_count, head_size)
        pair_view = pair_rows.reshape(seqs_dev, blk_rows, head_count, 2, head_size)
        raw_scores = (
            jnp.einsum(
                "bqhe,bkhe->bhqk", q_rows, pair_view[..., 0, :], preferred_element_type=jnp.float32
            )
            * score_scale
        )
        prob_full = jnp.exp(raw_scores - sent_stats[:, 0][..., None])
        grad_prob = jnp.einsum(
            "bqhe,bkhe->bhqk", do_rows, pair_view[..., 1, :], preferred_element_type=jnp.float32
        )
        dscore = (prob_full * (grad_prob - sent_stats[:, 1][..., None]) * score_scale).astype(
            jnp.bfloat16
        )
        key_grad = jnp.einsum("bhqk,bqhe->bkhe", dscore, q_rows, preferred_element_type=jnp.float32)
        value_grad = jnp.einsum(
            "bhqk,bqhe->bkhe",
            prob_full.astype(jnp.bfloat16),
            do_rows,
            preferred_element_type=jnp.float32,
        )
        return jnp.stack([key_grad, value_grad], 3).reshape(seqs_dev, blk_rows, pair_width)

    from_right = move_grads(fine_left_conv, -1)
    query_tail = jnp.concatenate([queries[:, -blk_rows:], grad_out[:, -blk_rows:]], 2)
    query_front = jnp.concatenate([queries[:, :blk_rows], grad_out[:, :blk_rows]], 2)
    stats_tail = jnp.stack([log_totals[:, -1], row_deltas[:, -1]], 1)
    stats_front = jnp.stack([log_totals[:, 0], row_deltas[:, 0]], 1)
    tail_from_left = move_near(query_tail, 1)
    front_from_right = move_near(query_front, -1)
    stats_from_left = move_grads(stats_tail, 1)
    stats_from_right = move_grads(stats_front, -1)
    left_terms = owner_terms(tail_from_left, stats_from_left, fine_pairs[:, :blk_rows])
    right_terms = owner_terms(front_from_right, stats_from_right, fine_pairs[:, -blk_rows:])
    fine_grad = (
        grad_own[0].at[:, :blk_rows].add(left_terms).at[:, -blk_rows:].add(right_terms + from_right)
    )
    grad_pairs = fine_grad.reshape(seqs_dev, tok_rows, head_count, 2, head_size)
    grad_key = (
        grad_pairs[:, :, :, 0, :].reshape(seqs_dev, tok_rows, feat_width).astype(jnp.bfloat16)
    )
    grad_value = (
        grad_pairs[:, :, :, 1, :].reshape(seqs_dev, tok_rows, feat_width).astype(jnp.bfloat16)
    )
    weight_sum = lax.psum(jnp.stack(weight_grads), ("seq", "dp")).reshape(
        levels, 4, head_count, 2, head_size
    )
    grad_conv_key = weight_sum[:, :, :, 0, :].reshape(levels, 4, feat_width)
    grad_conv_value = weight_sum[:, :, :, 1, :].reshape(levels, 4, feat_width)
    return (attended, grad_query, grad_key, grad_value, grad_conv_key, grad_conv_value)


LOG2E = 1.4426950408889634
MASKED = -1e30


def level_bases(blocks, levels):
    bases, offset = [], 0
    for level_id in range(levels + 1):
        bases.append(offset)
        offset += (blocks >> level_id) + 2
    return bases, offset


def build_levels(load_pair, weight, bases, blocks, levels, wide_ref, low_ref, turned_ref):
    zero_wide = jnp.zeros((BLOCK, HEAD_DIM), jnp.float32)
    zero_low = jnp.zeros((BLOCK, HEAD_DIM), jnp.bfloat16)
    for level_id in range(levels + 1):
        for pad in (bases[level_id], bases[level_id] + (blocks >> level_id) + 1):
            wide_ref[pad * BLOCK : (pad + 1) * BLOCK] = zero_wide
            low_ref[pad] = zero_low
            turned_ref[pad] = zero_low

    def put(index, low):
        wide = low.astype(jnp.float32)
        wide_ref[pl.ds(pl.multiple_of(index * BLOCK, BLOCK), BLOCK)] = wide
        low_ref[index] = low
        turned_ref[index] = wide.T.astype(jnp.bfloat16)

    def put_pair(pair, carry):
        rows = load_pair(pair)
        put(1 + 2 * pair, rows[:BLOCK])
        put(2 + 2 * pair, rows[BLOCK:])
        return carry

    lax.fori_loop(0, blocks // 2, put_pair, 0)
    for level_id in range(1, levels + 1):
        for block in range(blocks >> level_id):
            start = (bases[level_id - 1] + 1 + 2 * block) * BLOCK - 2
            summed = jnp.zeros((BLOCK, HEAD_DIM), jnp.float32)
            for tap in range(4):
                row = 4 * (level_id - 1) + tap
                summed = summed + weight(row) * wide_ref[pl.ds(start + tap, BLOCK, stride=2)]
            put(bases[level_id] + 1 + block, summed.astype(jnp.bfloat16))


def attend_pair(pair, q_rows, do_rows, bases, blocks, levels, keys, values, scratch):
    key_low, key_turned, key_grad = keys
    value_low, value_turned, value_grad = values
    score_ref, dprob_ref = scratch
    scale = HEAD_DIM**-0.5
    two = 2 * BLOCK
    q_turned = q_rows.astype(jnp.float32).T.astype(jnp.bfloat16)
    do_turned = do_rows.astype(jnp.float32).T.astype(jnp.bfloat16)
    lane = lax.broadcasted_iota(jnp.int32, (1, two), 1)
    pairs = blocks // 2
    places = [2 * pair, 2 * pair + 1, 2 * pair + 2, 2 * pair + 3]
    spans = [
        (0, jnp.where(pair > 0, BLOCK, 0)),
        None,
        None,
        (jnp.where(pair + 1 < pairs, BLOCK, two), two),
    ]
    for level_id in range(1, levels + 1):
        coarse_id = pair // 2 ** (level_id - 1)
        places += [bases[level_id] + coarse_id, bases[level_id] + coarse_id + 2]
        spans += [
            (0, jnp.where(coarse_id >= 1, two, 0)),
            (0, jnp.where(coarse_id + 1 < blocks >> level_id, two, 0)),
        ]
    row_max = jnp.full((1, two), MASKED, jnp.float32)
    for piece, place in enumerate(places):
        score = jnp.dot(key_low[place], q_turned, preferred_element_type=jnp.float32)
        if spans[piece] is not None:
            first, last = spans[piece]
            score = jnp.where((lane >= first) & (lane < last), score, MASKED)
        score_ref[piece] = score
        row_max = jnp.maximum(row_max, jnp.max(score, 0, keepdims=True))
    total = jnp.zeros((1, two), jnp.float32)
    weighted = jnp.zeros((1, two), jnp.float32)
    for piece, place in enumerate(places):
        raised = jnp.exp2((score_ref[piece] - row_max) * (scale * LOG2E))
        dprob = jnp.dot(value_low[place], do_turned, preferred_element_type=jnp.float32)
        score_ref[piece] = raised
        dprob_ref[piece] = dprob
        total = total + jnp.sum(raised, 0, keepdims=True)
        weighted = weighted + jnp.sum(raised * dprob, 0, keepdims=True)
    inverse = 1.0 / total
    delta = weighted * inverse
    attended = jnp.zeros((HEAD_DIM, two), jnp.float32)
    grad_q = jnp.zeros((HEAD_DIM, two), jnp.float32)
    for piece in range(0, len(places), 2):
        lows, dlows = [], []
        for step in (piece, piece + 1):
            rows = pl.ds(pl.multiple_of(places[step] * BLOCK, BLOCK), BLOCK)
            probs = score_ref[step] * inverse
            probs_low = probs.astype(jnp.bfloat16)
            dscore = (probs * (dprob_ref[step] - delta)).astype(jnp.bfloat16)
            value_grad[rows] += jnp.dot(probs_low, do_rows, preferred_element_type=jnp.float32)
            key_grad[rows] += jnp.dot(dscore, q_rows, preferred_element_type=jnp.float32)
            lows.append(probs_low)
            dlows.append(dscore)
        here, there = places[piece], places[piece + 1]
        value_two = jnp.concatenate([value_turned[here], value_turned[there]], 1)
        key_two = jnp.concatenate([key_turned[here], key_turned[there]], 1)
        attended = attended + jnp.dot(
            value_two, jnp.concatenate(lows, 0), preferred_element_type=jnp.float32
        )
        grad_q = grad_q + jnp.dot(
            key_two, jnp.concatenate(dlows, 0), preferred_element_type=jnp.float32
        )
    return attended.T.astype(jnp.bfloat16), (grad_q * scale).T.astype(jnp.bfloat16)


def coarsen_gradients(weight, bases, blocks, levels, wide_ref, grad_ref, put_weight_grad):
    for level_id in range(levels, 0, -1):
        tap_sums = [jnp.zeros((1, HEAD_DIM), jnp.float32) for _ in range(4)]
        for block in range(blocks >> level_id):
            start = (bases[level_id] + 1 + block) * BLOCK
            upstream = grad_ref[start : start + BLOCK]
            following = grad_ref[start + 1 : start + 1 + BLOCK]
            below = (bases[level_id - 1] + 1 + 2 * block) * BLOCK
            taps = [weight(4 * (level_id - 1) + tap) for tap in range(4)]
            grad_ref[pl.ds(below, BLOCK, stride=2)] += taps[2] * upstream + taps[0] * following
            grad_ref[pl.ds(below + 1, BLOCK, stride=2)] += taps[3] * upstream + taps[1] * following
            for tap in range(4):
                tap_sums[tap] = tap_sums[tap] + jnp.sum(
                    upstream * wide_ref[pl.ds(below - 2 + tap, BLOCK, stride=2)], 0, keepdims=True
                )
        for tap in range(4):
            put_weight_grad(4 * (level_id - 1) + tap, tap_sums[tap])


def head_kernel(
    levels,
    rows_ref,
    conv_ref,
    out_ref,
    conv_grad_ref,
    key_wide,
    key_low,
    key_turned,
    key_grad,
    value_wide,
    value_low,
    value_turned,
    value_grad,
    score_ref,
    dprob_ref,
):
    pairs = rows_ref.shape[0]
    blocks = 2 * pairs
    bases, _ = level_bases(blocks, levels)
    taps = 4 * levels
    scale = HEAD_DIM**-0.5

    def key_weight(row):
        return conv_ref[row : row + 1]

    def value_weight(row):
        return conv_ref[taps + row : taps + row + 1]

    shape = (bases, blocks, levels)
    build_levels(lambda pair: rows_ref[pair, 1], key_weight, *shape, key_wide, key_low, key_turned)
    build_levels(
        lambda pair: rows_ref[pair, 2], value_weight, *shape, value_wide, value_low, value_turned
    )
    key_grad[...] = jnp.zeros_like(key_grad)
    value_grad[...] = jnp.zeros_like(value_grad)

    def step(pair, carry):
        attended, grad_q = attend_pair(
            pair,
            rows_ref[pair, 0],
            rows_ref[pair, 3],
            *shape,
            (key_low, key_turned, key_grad),
            (value_low, value_turned, value_grad),
            (score_ref, dprob_ref),
        )
        out_ref[pair, 0] = attended
        out_ref[pair, 1] = grad_q
        return carry

    lax.fori_loop(0, pairs, step, 0)

    def put_key(row, value):
        conv_grad_ref[row : row + 1] = value * scale

    def put_value(row, value):
        conv_grad_ref[taps + row : taps + row + 1] = value

    coarsen_gradients(key_weight, *shape, key_wide, key_grad, put_key)
    coarsen_gradients(value_weight, *shape, value_wide, value_grad, put_value)

    def finish(pair, carry):
        rows = pl.ds(pl.multiple_of((1 + 2 * pair) * BLOCK, BLOCK), 2 * BLOCK)
        out_ref[pair, 2] = (key_grad[rows] * scale).astype(jnp.bfloat16)
        out_ref[pair, 3] = value_grad[rows].astype(jnp.bfloat16)
        return carry

    lax.fori_loop(0, pairs, finish, 0)


def stack_scratch(blocks, levels):
    total = level_bases(blocks, levels)[1]
    flat = pltpu.VMEM((total * BLOCK, HEAD_DIM), jnp.float32)
    low = pltpu.VMEM((total, BLOCK, HEAD_DIM), jnp.bfloat16)
    return [flat, low, low, flat]


def one_head(rows, conv, levels):
    pairs = rows.shape[0]
    pieces = 4 + 2 * levels
    scores = pltpu.VMEM((pieces, BLOCK, 2 * BLOCK), jnp.float32)
    return pl.pallas_call(
        functools.partial(head_kernel, levels),
        out_shape=(
            jax.ShapeDtypeStruct(rows.shape, jnp.bfloat16),
            jax.ShapeDtypeStruct(conv.shape, jnp.float32),
        ),
        in_specs=[pl.BlockSpec(memory_space=pltpu.VMEM)] * 2,
        out_specs=[pl.BlockSpec(memory_space=pltpu.VMEM)] * 2,
        scratch_shapes=stack_scratch(2 * pairs, levels) * 2 + [scores, scores],
        compiler_params=pltpu.CompilerParams(vmem_limit_bytes=48 * 2**20),
    )(rows, conv)


def per_device_heads(queries, key_rows, value_rows, conv_key, conv_value, grad_out):
    tok_rows = queries.shape[1]
    levels = conv_key.shape[0]
    head = lax.axis_index("seq")
    stacked = jnp.stack([queries[0], key_rows[0], value_rows[0], grad_out[0]])
    split = stacked.reshape(4, tok_rows, HEADS, HEAD_DIM).transpose(2, 0, 1, 3)
    rows = lax.all_to_all(split, "seq", 0, 0)
    conv = jnp.concatenate([conv_key, conv_value], 0).reshape(8 * levels, HEADS * HEAD_DIM)
    conv_here = lax.dynamic_slice_in_dim(conv, head * HEAD_DIM, HEAD_DIM, 1)
    outs, conv_grad = one_head(rows, conv_here, levels)
    back = lax.all_to_all(outs, "seq", 0, 0)
    whole = back.transpose(1, 2, 0, 3).reshape(4, 1, tok_rows, HEADS * HEAD_DIM)
    placed = lax.dynamic_update_slice_in_dim(
        jnp.zeros_like(conv), conv_grad, head * HEAD_DIM, 1
    )
    conv_sum = lax.psum(placed, ("seq", "dp")).reshape(2, levels, 4, HEADS * HEAD_DIM)
    return (whole[0], whole[1], whole[2], whole[3], conv_sum[0], conv_sum[1])


def solution(mesh):
    in_specs = (
        P("dp", "seq", None),
        P("dp", "seq", None),
        P("dp", "seq", None),
        P(),
        P(),
        P("dp", "seq", None),
    )
    out_specs = (
        P("dp", "seq", None),
        P("dp", "seq", None),
        P("dp", "seq", None),
        P("dp", "seq", None),
        P(),
        P(),
    )
    def chosen(*args):
        seq_devices = lax.axis_size("seq")
        fits = seq_devices == HEADS and args[0].shape[:2] == (1, 2 * BLOCK)
        return (per_device_heads if fits else per_device)(*args)

    return jax.shard_map(
        chosen, mesh=mesh, in_specs=in_specs, out_specs=out_specs, check_vma=False
    )
```

```python
import functools

import jax
import jax.numpy as jnp
from jax import lax
from jax.experimental import pallas as pl
from jax.experimental.pallas import tpu as pltpu
from jax.sharding import PartitionSpec as P

HEADS = 8
HEAD_DIM = 128
BLOCK = 128


def passed_along(value, axis, steps):
    count = lax.axis_size(axis)
    initial, last = (max(0, -steps), min(count, count - steps))
    return lax.ppermute(value, axis, [(source, source + steps) for source in range(initial, last)])


def partner_2(array, axis, distance):
    return lax.ppermute(array, axis, [(i, i ^ 1 << distance) for i in range(lax.axis_size(axis))])


def coarsen(extended, weight):
    out_rows = (extended.shape[1] - 2) // 2
    summed = weight[0] * extended[:, 0 : 2 * out_rows : 2].astype(jnp.float32)
    for offset in range(1, 4):
        summed = summed + weight[offset] * extended[:, offset : offset + 2 * out_rows : 2].astype(
            jnp.float32
        )
    return summed.astype(jnp.bfloat16)


def coarsen_back(upstream, extended, weight):
    seqs_dev, out_rows, feat_width = upstream.shape
    zero_row = jnp.zeros((seqs_dev, 1, feat_width), jnp.float32)
    even_rows = jnp.concatenate([weight[0] * upstream, zero_row], 1) + jnp.concatenate(
        [zero_row, weight[2] * upstream], 1
    )
    odd_rows = jnp.concatenate([weight[1] * upstream, zero_row], 1) + jnp.concatenate(
        [zero_row, weight[3] * upstream], 1
    )
    spread = jnp.stack([even_rows, odd_rows], 2).reshape(seqs_dev, 2 * out_rows + 2, feat_width)
    weight_grad = jnp.stack(
        [
            jnp.sum(
                upstream * extended[:, offset : offset + 2 * out_rows : 2].astype(jnp.float32),
                (0, 1),
            )
            for offset in range(4)
        ]
    )
    return (spread, weight_grad)


def move_near(moved_rows, shift_by):
    return passed_along(moved_rows, "seq", shift_by)


def move_grads(moved_rows, shift_by):
    return passed_along(moved_rows.astype(jnp.bfloat16), "seq", shift_by).astype(moved_rows.dtype)


def per_device(queries, key_rows, value_rows, conv_key, conv_value, grad_out):
    seqs_dev, tok_rows, feat_width = queries.shape
    levels = conv_key.shape[0]
    head_count = HEADS
    head_size = HEAD_DIM
    blk_rows = BLOCK
    blocks_here = tok_rows // blk_rows
    local_top = blocks_here.bit_length() - 1
    seq_devices = lax.axis_size("seq")
    dev_index = lax.axis_index("seq")
    total_blocks = blocks_here * seq_devices
    score_scale = head_size ** (-0.5)
    pair_width = 2 * feat_width
    group_heads = 2
    kv_weight = jnp.stack(
        [
            conv_key.reshape(levels, 4, head_count, head_size),
            conv_value.reshape(levels, 4, head_count, head_size),
        ],
        3,
    ).reshape(levels, 4, pair_width)
    fine_pairs = jnp.stack(
        [
            key_rows.reshape(seqs_dev, tok_rows, head_count, head_size),
            value_rows.reshape(seqs_dev, tok_rows, head_count, head_size),
        ],
        3,
    ).reshape(seqs_dev, tok_rows, pair_width)
    own_rows = [fine_pairs]
    left_rims = [move_near(fine_pairs[:, -blk_rows:], 1)]
    right_rims = [move_near(fine_pairs[:, :blk_rows], -1)]
    extended_local = [None]
    level_id = 1
    extended = jnp.concatenate([left_rims[level_id - 1][:, -2:], own_rows[level_id - 1]], 1)
    extended_local.append(extended)
    coarse = coarsen(extended, kv_weight[level_id - 1])
    own_rows.append(coarse)
    left_rims.append(move_near(coarse, 1))
    right_rims.append(move_near(coarse, -1))
    block_now = own_rows[local_top]
    left_now = left_rims[local_top]
    group_lefts, group_rights, group_extended, group_first = ([], [], [], [])
    for level_id in range(local_top + 1, levels + 1):
        swap_bit = level_id - local_top - 1
        extended = jnp.concatenate([left_now[:, -2:], block_now], 1)
        group_extended.append(extended)
        own_half = coarsen(extended, kv_weight[level_id - 1])
        partner = partner_2(own_half, "seq", swap_bit)
        is_first = dev_index // 2**swap_bit % 2 == 0
        group_first.append(is_first)
        block_now = jnp.where(
            is_first,
            jnp.concatenate([own_half, partner], 1),
            jnp.concatenate([partner, own_half], 1),
        )
        stride_dev = 2 ** (level_id - local_top)
        left_now = move_near(block_now, stride_dev)
        right_now = move_near(block_now, -stride_dev)
        group_lefts.append(left_now)
        group_rights.append(right_now)
    glob_blocks = dev_index * blocks_here + jnp.arange(blocks_here, dtype=jnp.int32)
    always = jnp.ones((blocks_here,), jnp.bool_)
    sources = []
    pieces = []
    for level_id in range(local_top + 1):
        block_count = blocks_here >> level_id
        padded = jnp.concatenate([left_rims[level_id], own_rows[level_id], right_rims[level_id]], 1)
        sources.append(
            padded.reshape(seqs_dev, block_count + 2, blk_rows, head_count, 2, head_size)
        )
        coarse_id = glob_blocks // 2**level_id
        spread = 2**level_id
        pieces.append((level_id, 0, spread, coarse_id >= 1))
        if level_id == 0:
            pieces.append((0, 1, 1, always))
        pieces.append((level_id, 2, spread, coarse_id + 1 < total_blocks // 2**level_id))
    for slot_id in range(levels - local_top):
        level_id = local_top + 1 + slot_id
        coarse_id = glob_blocks // 2**level_id
        sources.append(
            group_lefts[slot_id].reshape(seqs_dev, 1, blk_rows, head_count, 2, head_size)
        )
        pieces.append((len(sources) - 1, 0, blocks_here, coarse_id >= 1))
        sources.append(
            group_rights[slot_id].reshape(seqs_dev, 1, blk_rows, head_count, 2, head_size)
        )
        pieces.append(
            (len(sources) - 1, 0, blocks_here, coarse_id + 1 < total_blocks // 2**level_id)
        )
    query_blocks = queries.reshape(seqs_dev, blocks_here, blk_rows, head_count, head_size)
    out_blocks = grad_out.reshape(seqs_dev, blocks_here, blk_rows, head_count, head_size)

    def head_group(group_id, loop_state):
        attended_acc, grad_q_acc, source_grads, log_totals, row_deltas = loop_state
        head_start = group_id * group_heads
        q_part = lax.dynamic_slice_in_dim(query_blocks, head_start, group_heads, 3)
        do_part = lax.dynamic_slice_in_dim(out_blocks, head_start, group_heads, 3)
        source_parts = [
            lax.dynamic_slice_in_dim(source, head_start, group_heads, 3) for source in sources
        ]
        score_list = []
        views = []
        for source_id, offset, spread, valid_mask in pieces:
            block_count = blocks_here // spread
            key_blocks = source_parts[source_id][:, offset : offset + block_count]
            q_view = q_part.reshape(seqs_dev, block_count, spread, blk_rows, group_heads, head_size)
            do_view = do_part.reshape(
                seqs_dev, block_count, spread, blk_rows, group_heads, head_size
            )
            raw_scores = jnp.einsum(
                "bnrqhe,bnkhe->bnrhqk",
                q_view,
                key_blocks[..., 0, :],
                preferred_element_type=jnp.float32,
            )
            raw_scores = (
                raw_scores.reshape(seqs_dev, blocks_here, group_heads, blk_rows, blk_rows)
                * score_scale
            )
            score_list.append(
                jnp.where(valid_mask[None, :, None, None, None], raw_scores, -jnp.inf)
            )
            views.append((key_blocks, q_view, do_view, block_count, spread))
        all_scores = jnp.concatenate(score_list, 4)
        row_max = jnp.max(all_scores, 4, keepdims=True)
        exp_scores = jnp.exp(all_scores - row_max)
        summed = jnp.sum(exp_scores, 4, keepdims=True)
        prob_full = exp_scores / summed
        probs_low = prob_full.astype(jnp.bfloat16)
        attended_part = jnp.zeros(
            (seqs_dev, blocks_here, blk_rows, group_heads, head_size), jnp.float32
        )
        grad_prob_list = []
        for piece_id, (key_blocks, q_view, do_view, block_count, spread) in enumerate(views):
            p_slice = probs_low[..., piece_id * blk_rows : (piece_id + 1) * blk_rows].reshape(
                seqs_dev, block_count, spread, group_heads, blk_rows, blk_rows
            )
            attended_part = attended_part + jnp.einsum(
                "bnrhqk,bnkhe->bnrqhe",
                p_slice,
                key_blocks[..., 1, :],
                preferred_element_type=jnp.float32,
            ).reshape(attended_part.shape)
            grad_prob = jnp.einsum(
                "bnrqhe,bnkhe->bnrhqk",
                do_view,
                key_blocks[..., 1, :],
                preferred_element_type=jnp.float32,
            )
            grad_prob_list.append(
                grad_prob.reshape(seqs_dev, blocks_here, group_heads, blk_rows, blk_rows)
            )
        grad_prob_all = jnp.concatenate(grad_prob_list, 4)
        row_delta = jnp.sum(prob_full * grad_prob_all, 4, keepdims=True)
        dscore = (prob_full * (grad_prob_all - row_delta) * score_scale).astype(jnp.bfloat16)
        grad_q_part = jnp.zeros(
            (seqs_dev, blocks_here, blk_rows, group_heads, head_size), jnp.float32
        )
        group_grads = [jnp.zeros(part_arr.shape, jnp.float32) for part_arr in source_parts]
        for piece_id, (key_blocks, q_view, do_view, block_count, spread) in enumerate(views):
            source_id, offset = (pieces[piece_id][0], pieces[piece_id][1])
            p_slice = probs_low[..., piece_id * blk_rows : (piece_id + 1) * blk_rows].reshape(
                seqs_dev, block_count, spread, group_heads, blk_rows, blk_rows
            )
            ds_slice = dscore[..., piece_id * blk_rows : (piece_id + 1) * blk_rows].reshape(
                seqs_dev, block_count, spread, group_heads, blk_rows, blk_rows
            )
            grad_q_part = grad_q_part + jnp.einsum(
                "bnrhqk,bnkhe->bnrqhe",
                ds_slice,
                key_blocks[..., 0, :],
                preferred_element_type=jnp.float32,
            ).reshape(grad_q_part.shape)
            key_grad = jnp.einsum(
                "bnrhqk,bnrqhe->bnkhe", ds_slice, q_view, preferred_element_type=jnp.float32
            )
            value_grad = jnp.einsum(
                "bnrhqk,bnrqhe->bnkhe", p_slice, do_view, preferred_element_type=jnp.float32
            )
            pair_grad = jnp.stack([key_grad, value_grad], 4)
            group_grads[source_id] = (
                group_grads[source_id].at[:, offset : offset + block_count].add(pair_grad)
            )
        attended_acc = lax.dynamic_update_slice_in_dim(
            attended_acc, attended_part.astype(jnp.bfloat16), head_start, 3
        )
        grad_q_acc = lax.dynamic_update_slice_in_dim(
            grad_q_acc, grad_q_part.astype(jnp.bfloat16), head_start, 3
        )
        source_grads = tuple(
            (
                lax.dynamic_update_slice_in_dim(whole, group_part, head_start, 3)
                for whole, group_part in zip(source_grads, group_grads)
            )
        )
        log_totals = lax.dynamic_update_slice_in_dim(
            log_totals, (row_max + jnp.log(summed))[..., 0], head_start, 2
        )
        row_deltas = lax.dynamic_update_slice_in_dim(row_deltas, row_delta[..., 0], head_start, 2)
        return (attended_acc, grad_q_acc, source_grads, log_totals, row_deltas)

    start_state = (
        jnp.zeros((seqs_dev, blocks_here, blk_rows, head_count, head_size), jnp.bfloat16),
        jnp.zeros((seqs_dev, blocks_here, blk_rows, head_count, head_size), jnp.bfloat16),
        tuple((jnp.zeros(source.shape, jnp.float32) for source in sources)),
        jnp.zeros((seqs_dev, blocks_here, head_count, blk_rows), jnp.float32),
        jnp.zeros((seqs_dev, blocks_here, head_count, blk_rows), jnp.float32),
    )
    attended_acc, grad_q_acc, source_grads, log_totals, row_deltas = lax.fori_loop(
        0, head_count // group_heads, head_group, start_state
    )
    attended = attended_acc.reshape(seqs_dev, tok_rows, feat_width)
    grad_query = grad_q_acc.reshape(seqs_dev, tok_rows, feat_width)
    grad_left, grad_own, grad_right = ([], [], [])
    for level_id in range(local_top + 1):
        flat_grad = source_grads[level_id].reshape(seqs_dev, -1, pair_width)
        grad_left.append(flat_grad[:, :blk_rows])
        grad_own.append(flat_grad[:, blk_rows:-blk_rows])
        grad_right.append(flat_grad[:, -blk_rows:])
    group_left_grads = [
        source_grads[local_top + 1 + 2 * slot_id].reshape(seqs_dev, blk_rows, pair_width)
        for slot_id in range(levels - local_top)
    ]
    group_right_grads = [
        source_grads[local_top + 2 + 2 * slot_id].reshape(seqs_dev, blk_rows, pair_width)
        for slot_id in range(levels - local_top)
    ]
    weight_grads = [None] * levels
    carry_block = jnp.zeros((seqs_dev, blk_rows, pair_width), jnp.float32)
    carry_left = jnp.zeros((seqs_dev, 2, pair_width), jnp.float32)
    for level_id in range(levels, local_top, -1):
        slot_id = level_id - local_top - 1
        stride_dev = 2 ** (level_id - local_top)
        left_total = group_left_grads[slot_id].at[:, -2:].add(carry_left)
        block_total = (
            carry_block
            + move_grads(left_total, -stride_dev)
            + move_grads(group_right_grads[slot_id], stride_dev)
        )
        first_part = block_total[:, : blk_rows // 2]
        second_part = block_total[:, blk_rows // 2 :]
        keep_part = jnp.where(group_first[slot_id], first_part, second_part)
        give_part = jnp.where(group_first[slot_id], second_part, first_part)
        half_grad = keep_part + partner_2(give_part.astype(jnp.bfloat16), "seq", slot_id).astype(
            give_part.dtype
        )
        spread, weight_grads[level_id - 1] = coarsen_back(
            half_grad, group_extended[slot_id], kv_weight[level_id - 1]
        )
        carry_left = spread[:, :2]
        carry_block = spread[:, 2:]
    grad_left[local_top] = grad_left[local_top].at[:, -2:].add(carry_left)
    grad_own[local_top] = grad_own[local_top] + carry_block
    fine_left_conv = jnp.zeros((seqs_dev, blk_rows, pair_width), jnp.float32)
    level_id = 1
    from_right = move_grads(grad_left[level_id], -1)
    from_left = move_grads(grad_right[level_id], 1)
    level_grad = (
        grad_own[level_id].at[:, :blk_rows].add(from_left).at[:, -blk_rows:].add(from_right)
    )
    spread, weight_grads[level_id - 1] = coarsen_back(
        level_grad, extended_local[level_id], kv_weight[level_id - 1]
    )
    fine_left_conv = fine_left_conv.at[:, -2:].add(spread[:, :2])
    grad_own[level_id - 1] = grad_own[level_id - 1] + spread[:, 2:]

    def owner_terms(sent_rows, sent_stats, pair_rows):
        q_rows = sent_rows[:, :, :feat_width].reshape(seqs_dev, blk_rows, head_count, head_size)
        do_rows = sent_rows[:, :, feat_width:].reshape(seqs_dev, blk_rows, head_count, head_size)
        pair_view = pair_rows.reshape(seqs_dev, blk_rows, head_count, 2, head_size)
        raw_scores = (
            jnp.einsum(
                "bqhe,bkhe->bhqk", q_rows, pair_view[..., 0, :], preferred_element_type=jnp.float32
            )
            * score_scale
        )
        prob_full = jnp.exp(raw_scores - sent_stats[:, 0][..., None])
        grad_prob = jnp.einsum(
            "bqhe,bkhe->bhqk", do_rows, pair_view[..., 1, :], preferred_element_type=jnp.float32
        )
        dscore = (prob_full * (grad_prob - sent_stats[:, 1][..., None]) * score_scale).astype(
            jnp.bfloat16
        )
        key_grad = jnp.einsum("bhqk,bqhe->bkhe", dscore, q_rows, preferred_element_type=jnp.float32)
        value_grad = jnp.einsum(
            "bhqk,bqhe->bkhe",
            prob_full.astype(jnp.bfloat16),
            do_rows,
            preferred_element_type=jnp.float32,
        )
        return jnp.stack([key_grad, value_grad], 3).reshape(seqs_dev, blk_rows, pair_width)

    from_right = move_grads(fine_left_conv, -1)
    query_tail = jnp.concatenate([queries[:, -blk_rows:], grad_out[:, -blk_rows:]], 2)
    query_front = jnp.concatenate([queries[:, :blk_rows], grad_out[:, :blk_rows]], 2)
    stats_tail = jnp.stack([log_totals[:, -1], row_deltas[:, -1]], 1)
    stats_front = jnp.stack([log_totals[:, 0], row_deltas[:, 0]], 1)
    tail_from_left = move_near(query_tail, 1)
    front_from_right = move_near(query_front, -1)
    stats_from_left = move_grads(stats_tail, 1)
    stats_from_right = move_grads(stats_front, -1)
    left_terms = owner_terms(tail_from_left, stats_from_left, fine_pairs[:, :blk_rows])
    right_terms = owner_terms(front_from_right, stats_from_right, fine_pairs[:, -blk_rows:])
    fine_grad = (
        grad_own[0].at[:, :blk_rows].add(left_terms).at[:, -blk_rows:].add(right_terms + from_right)
    )
    grad_pairs = fine_grad.reshape(seqs_dev, tok_rows, head_count, 2, head_size)
    grad_key = (
        grad_pairs[:, :, :, 0, :].reshape(seqs_dev, tok_rows, feat_width).astype(jnp.bfloat16)
    )
    grad_value = (
        grad_pairs[:, :, :, 1, :].reshape(seqs_dev, tok_rows, feat_width).astype(jnp.bfloat16)
    )
    weight_sum = lax.psum(jnp.stack(weight_grads), ("seq", "dp")).reshape(
        levels, 4, head_count, 2, head_size
    )
    grad_conv_key = weight_sum[:, :, :, 0, :].reshape(levels, 4, feat_width)
    grad_conv_value = weight_sum[:, :, :, 1, :].reshape(levels, 4, feat_width)
    return (attended, grad_query, grad_key, grad_value, grad_conv_key, grad_conv_value)


LOG2E = 1.4426950408889634
MASKED = -1e30


def level_bases(blocks, levels):
    bases, offset = [], 0
    for level_id in range(levels + 1):
        bases.append(offset)
        offset += (blocks >> level_id) + 2
    return bases, offset


def build_levels(take_rows, weight, bases, blocks, levels, wide_ref, low_ref, turned_ref):
    zero_wide = jnp.zeros((BLOCK, HEAD_DIM), jnp.float32)
    zero_low = jnp.zeros((BLOCK, HEAD_DIM), jnp.bfloat16)
    for level_id in range(levels + 1):
        for pad in (bases[level_id], bases[level_id] + (blocks >> level_id) + 1):
            wide_ref[pad * BLOCK : (pad + 1) * BLOCK] = zero_wide
            low_ref[pad] = zero_low
            turned_ref[pad] = zero_low

    def put(index, low):
        wide = low.astype(jnp.float32)
        wide_ref[pl.ds(pl.multiple_of(index * BLOCK, BLOCK), BLOCK)] = wide
        low_ref[index] = low
        turned_ref[index] = wide.T.astype(jnp.bfloat16)

    def put_pair(distance, carry):
        pair, rows = take_rows(distance)
        put(1 + 2 * pair, rows[:BLOCK])
        put(2 + 2 * pair, rows[BLOCK:])
        return carry

    lax.fori_loop(0, blocks // 2, put_pair, 0)
    for level_id in range(1, levels + 1):
        for block in range(blocks >> level_id):
            start = (bases[level_id - 1] + 1 + 2 * block) * BLOCK - 2
            summed = jnp.zeros((BLOCK, HEAD_DIM), jnp.float32)
            for tap in range(4):
                row = 4 * (level_id - 1) + tap
                summed = summed + weight(row) * wide_ref[pl.ds(start + tap, BLOCK, stride=2)]
            put(bases[level_id] + 1 + block, summed.astype(jnp.bfloat16))


def attend_pair(pair, q_rows, do_rows, bases, blocks, levels, keys, values, scratch):
    key_low, key_turned, key_grad = keys
    value_low, value_turned, value_grad = values
    score_ref, dprob_ref = scratch
    scale = HEAD_DIM**-0.5
    two = 2 * BLOCK
    q_turned = q_rows.astype(jnp.float32).T.astype(jnp.bfloat16)
    do_turned = do_rows.astype(jnp.float32).T.astype(jnp.bfloat16)
    lane = lax.broadcasted_iota(jnp.int32, (1, two), 1)
    pairs = blocks // 2
    places = [2 * pair, 2 * pair + 1, 2 * pair + 2, 2 * pair + 3]
    spans = [
        (0, jnp.where(pair > 0, BLOCK, 0)),
        None,
        None,
        (jnp.where(pair + 1 < pairs, BLOCK, two), two),
    ]
    for level_id in range(1, levels + 1):
        coarse_id = pair // 2 ** (level_id - 1)
        places += [bases[level_id] + coarse_id, bases[level_id] + coarse_id + 2]
        spans += [
            (0, jnp.where(coarse_id >= 1, two, 0)),
            (0, jnp.where(coarse_id + 1 < blocks >> level_id, two, 0)),
        ]
    row_max = jnp.full((1, two), MASKED, jnp.float32)
    for piece, place in enumerate(places):
        score = jnp.dot(key_low[place], q_turned, preferred_element_type=jnp.float32)
        if spans[piece] is not None:
            first, last = spans[piece]
            score = jnp.where((lane >= first) & (lane < last), score, MASKED)
        score_ref[piece] = score
        row_max = jnp.maximum(row_max, jnp.max(score, 0, keepdims=True))
    total = jnp.zeros((1, two), jnp.float32)
    weighted = jnp.zeros((1, two), jnp.float32)
    for piece, place in enumerate(places):
        raised = jnp.exp2((score_ref[piece] - row_max) * (scale * LOG2E))
        dprob = jnp.dot(value_low[place], do_turned, preferred_element_type=jnp.float32)
        score_ref[piece] = raised
        dprob_ref[piece] = dprob
        total = total + jnp.sum(raised, 0, keepdims=True)
        weighted = weighted + jnp.sum(raised * dprob, 0, keepdims=True)
    inverse = 1.0 / total
    delta = weighted * inverse
    attended = jnp.zeros((HEAD_DIM, two), jnp.float32)
    grad_q = jnp.zeros((HEAD_DIM, two), jnp.float32)
    for piece in range(0, len(places), 2):
        lows, dlows = [], []
        for step in (piece, piece + 1):
            rows = pl.ds(pl.multiple_of(places[step] * BLOCK, BLOCK), BLOCK)
            probs = score_ref[step] * inverse
            probs_low = probs.astype(jnp.bfloat16)
            dscore = (probs * (dprob_ref[step] - delta)).astype(jnp.bfloat16)
            value_grad[rows] += jnp.dot(probs_low, do_rows, preferred_element_type=jnp.float32)
            key_grad[rows] += jnp.dot(dscore, q_rows, preferred_element_type=jnp.float32)
            lows.append(probs_low)
            dlows.append(dscore)
        here, there = places[piece], places[piece + 1]
        value_two = jnp.concatenate([value_turned[here], value_turned[there]], 1)
        key_two = jnp.concatenate([key_turned[here], key_turned[there]], 1)
        attended = attended + jnp.dot(
            value_two, jnp.concatenate(lows, 0), preferred_element_type=jnp.float32
        )
        grad_q = grad_q + jnp.dot(
            key_two, jnp.concatenate(dlows, 0), preferred_element_type=jnp.float32
        )
    return attended.T.astype(jnp.bfloat16), (grad_q * scale).T.astype(jnp.bfloat16)


def coarsen_gradients(weight, bases, blocks, levels, wide_ref, grad_ref, put_weight_grad):
    for level_id in range(levels, 0, -1):
        tap_sums = [jnp.zeros((1, HEAD_DIM), jnp.float32) for _ in range(4)]
        for block in range(blocks >> level_id):
            start = (bases[level_id] + 1 + block) * BLOCK
            upstream = grad_ref[start : start + BLOCK]
            following = grad_ref[start + 1 : start + 1 + BLOCK]
            below = (bases[level_id - 1] + 1 + 2 * block) * BLOCK
            taps = [weight(4 * (level_id - 1) + tap) for tap in range(4)]
            grad_ref[pl.ds(below, BLOCK, stride=2)] += taps[2] * upstream + taps[0] * following
            grad_ref[pl.ds(below + 1, BLOCK, stride=2)] += taps[3] * upstream + taps[1] * following
            for tap in range(4):
                tap_sums[tap] = tap_sums[tap] + jnp.sum(
                    upstream * wide_ref[pl.ds(below - 2 + tap, BLOCK, stride=2)], 0, keepdims=True
                )
        for tap in range(4):
            put_weight_grad(4 * (level_id - 1) + tap, tap_sums[tap])


def columns(head):
    return pl.ds(pl.multiple_of(head * HEAD_DIM, HEAD_DIM), HEAD_DIM)


def head_kernel(
    levels,
    ring,
    groups,
    q_hbm,
    key_hbm,
    value_hbm,
    do_hbm,
    conv_ref,
    att_hbm,
    grad_q_hbm,
    grad_key_hbm,
    grad_value_hbm,
    conv_grad_ref,
    rows_ref,
    out_ref,
    conv_here,
    conv_parts,
    conv_total,
    key_wide,
    key_low,
    key_turned,
    key_grad,
    value_wide,
    value_low,
    value_turned,
    value_grad,
    score_ref,
    dprob_ref,
    in_send,
    in_recv,
    out_send,
    out_recv,
    part_send,
    part_recv,
    total_send,
    total_recv,
):
    me = lax.axis_index("seq")
    group = lax.axis_index("dp")
    blocks = 2 * ring
    bases, _ = level_bases(blocks, levels)
    taps = 4 * levels
    scale = HEAD_DIM**-0.5
    sources = (q_hbm, key_hbm, value_hbm, do_hbm)
    results = (att_hbm, grad_q_hbm, grad_key_hbm, grad_value_hbm)

    def after(distance):
        return lax.rem(me + distance, ring)

    def before(distance):
        return lax.rem(me + ring - distance, ring)

    barrier = pltpu.get_barrier_semaphore()
    for distance in range(1, ring):
        pl.semaphore_signal(
            barrier,
            inc=1,
            device_id={"seq": after(distance)},
            device_id_type=pl.DeviceIdType.MESH,
        )
    for distance in range(1, groups):
        pl.semaphore_signal(
            barrier,
            inc=1,
            device_id={"dp": lax.rem(group + distance, groups)},
            device_id_type=pl.DeviceIdType.MESH,
        )
    pl.semaphore_wait(barrier, ring + groups - 2)

    def inbound(array, distance, landing):
        return pltpu.make_async_remote_copy(
            src_ref=sources[array].at[0, :, columns(after(distance))],
            dst_ref=rows_ref.at[landing, array],
            send_sem=in_send.at[array, distance],
            recv_sem=in_recv.at[array, distance],
            device_id={"seq": after(distance)},
            device_id_type=pl.DeviceIdType.MESH,
        )

    def inbound_own(array):
        return pltpu.make_async_copy(
            sources[array].at[0, :, columns(me)], rows_ref.at[me, array], in_recv.at[array, 0]
        )

    def outbound(array, distance, origin):
        return pltpu.make_async_remote_copy(
            src_ref=out_ref.at[before(distance), array],
            dst_ref=results[array].at[0, :, columns(origin)],
            send_sem=out_send.at[array, distance],
            recv_sem=out_recv.at[array, distance],
            device_id={"seq": before(distance)},
            device_id_type=pl.DeviceIdType.MESH,
        )

    def outbound_own(array):
        return pltpu.make_async_copy(
            out_ref.at[me, array], results[array].at[0, :, columns(me)], out_recv.at[array, 0]
        )

    for arrays in ((1,), (2,), (0, 3)):
        for array in arrays:
            inbound_own(array).start()

        def send(distance, carry, arrays=arrays):
            for array in arrays:
                inbound(array, distance, me).start()
            return carry

        lax.fori_loop(1, ring, send, 0)

    conv_here[...] = conv_ref[:, columns(me)]

    def arrived(array, distance):
        @pl.when(distance == 0)
        def _():
            inbound_own(array).wait()

        @pl.when(distance > 0)
        def _():
            inbound(array, distance, before(distance)).wait_recv()

    def leave(array, distance):
        @pl.when(distance == 0)
        def _():
            outbound_own(array).start()

        @pl.when(distance > 0)
        def _():
            outbound(array, distance, me).start()

    def taker(array):
        def take_rows(distance):
            arrived(array, distance)
            return before(distance), rows_ref[before(distance), array]

        return take_rows

    def key_weight(row):
        return conv_here[row : row + 1]

    def value_weight(row):
        return conv_here[taps + row : taps + row + 1]

    shape = (bases, blocks, levels)
    key_grad[...] = jnp.zeros_like(key_grad)
    value_grad[...] = jnp.zeros_like(value_grad)
    build_levels(taker(1), key_weight, *shape, key_wide, key_low, key_turned)
    build_levels(taker(2), value_weight, *shape, value_wide, value_low, value_turned)

    def step(distance, carry):
        pair = before(distance)
        arrived(0, distance)
        arrived(3, distance)
        attended, grad_q = attend_pair(
            pair,
            rows_ref[pair, 0],
            rows_ref[pair, 3],
            *shape,
            (key_low, key_turned, key_grad),
            (value_low, value_turned, value_grad),
            (score_ref, dprob_ref),
        )
        out_ref[pair, 0] = attended
        out_ref[pair, 1] = grad_q
        leave(0, distance)
        leave(1, distance)
        return carry

    lax.fori_loop(0, ring, step, 0)

    def put_key(row, value):
        conv_total[row : row + 1] = value * scale

    def put_value(row, value):
        conv_total[taps + row : taps + row + 1] = value

    def finisher(array, grad_ref, factor):
        def finish(distance, carry):
            pair = before(distance)
            rows = pl.ds(pl.multiple_of((1 + 2 * pair) * BLOCK, BLOCK), 2 * BLOCK)
            out_ref[pair, array] = (grad_ref[rows] * factor).astype(jnp.bfloat16)
            leave(array, distance)
            return carry

        return finish

    coarsen_gradients(key_weight, *shape, key_wide, key_grad, put_key)
    lax.fori_loop(0, ring, finisher(2, key_grad, scale), 0)
    coarsen_gradients(value_weight, *shape, value_wide, value_grad, put_value)

    def part(distance, slot):
        other = lax.rem(group + distance, groups)
        return pltpu.make_async_remote_copy(
            src_ref=conv_parts.at[group],
            dst_ref=conv_parts.at[slot],
            send_sem=part_send.at[distance],
            recv_sem=part_recv.at[distance],
            device_id={"dp": other},
            device_id_type=pl.DeviceIdType.MESH,
        )

    def gathered(distance, head):
        return pltpu.make_async_remote_copy(
            src_ref=conv_total,
            dst_ref=conv_grad_ref.at[:, columns(head)],
            send_sem=total_send.at[distance],
            recv_sem=total_recv.at[distance],
            device_id={"seq": after(distance)},
            device_id_type=pl.DeviceIdType.MESH,
        )

    conv_parts[group] = conv_total[...]
    for distance in range(1, groups):
        part(distance, group).start()
    lax.fori_loop(0, ring, finisher(3, value_grad, 1.0), 0)
    for distance in range(1, groups):
        part(distance, lax.rem(group + groups - distance, groups)).wait_recv()
    conv_sum = conv_parts[0]
    for slot in range(1, groups):
        conv_sum = conv_sum + conv_parts[slot]
    conv_total[...] = conv_sum
    conv_grad_ref[:, columns(me)] = conv_sum
    for distance in range(1, ring):
        gathered(distance, me).start()

    for array in range(4):
        outbound_own(array).wait()

    def settle(distance, carry):
        for array in range(4):
            inbound(array, distance, me).wait_send()
            outbound(array, distance, me).wait_send()
            outbound(array, distance, after(distance)).wait_recv()
        gathered(distance, me).wait_send()
        gathered(distance, before(distance)).wait_recv()
        return carry

    lax.fori_loop(1, ring, settle, 0)
    for distance in range(1, groups):
        part(distance, group).wait_send()


def stack_scratch(blocks, levels):
    total = level_bases(blocks, levels)[1]
    flat = pltpu.VMEM((total * BLOCK, HEAD_DIM), jnp.float32)
    low = pltpu.VMEM((total, BLOCK, HEAD_DIM), jnp.bfloat16)
    return [flat, low, low, flat]


def per_device_heads(queries, key_rows, value_rows, conv_key, conv_value, grad_out):
    tok_rows, feat_width = queries.shape[1:]
    levels = conv_key.shape[0]
    ring, groups = lax.axis_size("seq"), lax.axis_size("dp")
    conv = jnp.concatenate([conv_key, conv_value], 0).reshape(8 * levels, feat_width)
    like = jax.ShapeDtypeStruct(queries.shape, jnp.bfloat16)
    scores = pltpu.VMEM((4 + 2 * levels, BLOCK, 2 * BLOCK), jnp.float32)
    rows = pltpu.VMEM((ring, 4, tok_rows, HEAD_DIM), jnp.bfloat16)
    small = pltpu.VMEM((8 * levels, HEAD_DIM), jnp.float32)
    dma = pltpu.SemaphoreType.DMA
    anywhere = pl.BlockSpec(memory_space=pl.ANY)
    in_vmem = pl.BlockSpec(memory_space=pltpu.VMEM)
    outs = pl.pallas_call(
        functools.partial(head_kernel, levels, ring, groups),
        out_shape=(like, like, like, like, jax.ShapeDtypeStruct(conv.shape, jnp.float32)),
        in_specs=[anywhere] * 4 + [in_vmem],
        out_specs=[anywhere] * 4 + [in_vmem],
        scratch_shapes=[
            rows,
            rows,
            small,
            pltpu.VMEM((groups, 8 * levels, HEAD_DIM), jnp.float32),
            small,
        ]
        + stack_scratch(2 * ring, levels) * 2
        + [scores, scores]
        + [dma((4, ring))] * 4
        + [dma((groups,))] * 2
        + [dma((ring,))] * 2,
        compiler_params=pltpu.CompilerParams(
            collective_id=0, has_side_effects=True, vmem_limit_bytes=48 * 2**20
        ),
    )(queries, key_rows, value_rows, grad_out, conv)
    conv_sum = outs[4].reshape(2, levels, 4, feat_width)
    return (outs[0], outs[1], outs[2], outs[3], conv_sum[0], conv_sum[1])


def solution(mesh):
    in_specs = (
        P("dp", "seq", None),
        P("dp", "seq", None),
        P("dp", "seq", None),
        P(),
        P(),
        P("dp", "seq", None),
    )
    out_specs = (
        P("dp", "seq", None),
        P("dp", "seq", None),
        P("dp", "seq", None),
        P("dp", "seq", None),
        P(),
        P(),
    )
    def chosen(*args):
        seq_devices = lax.axis_size("seq")
        fits = seq_devices == HEADS and args[0].shape[:2] == (1, 2 * BLOCK)
        return (per_device_heads if fits else per_device)(*args)

    return jax.shard_map(
        chosen, mesh=mesh, in_specs=in_specs, out_specs=out_specs, check_vma=False
    )
```

```python
import functools

import jax
import jax.numpy as jnp
from jax import lax
from jax.experimental import pallas as pl
from jax.experimental.pallas import tpu as pltpu
from jax.sharding import PartitionSpec as P

HEADS = 8
HEAD_DIM = 128
BLOCK = 128


def passed_along(value, axis, steps):
    count = lax.axis_size(axis)
    initial, last = (max(0, -steps), min(count, count - steps))
    return lax.ppermute(value, axis, [(source, source + steps) for source in range(initial, last)])


def partner_2(array, axis, distance):
    return lax.ppermute(array, axis, [(i, i ^ 1 << distance) for i in range(lax.axis_size(axis))])


def coarsen(extended, weight):
    out_rows = (extended.shape[1] - 2) // 2
    summed = weight[0] * extended[:, 0 : 2 * out_rows : 2].astype(jnp.float32)
    for offset in range(1, 4):
        summed = summed + weight[offset] * extended[:, offset : offset + 2 * out_rows : 2].astype(
            jnp.float32
        )
    return summed.astype(jnp.bfloat16)


def coarsen_back(upstream, extended, weight):
    seqs_dev, out_rows, feat_width = upstream.shape
    zero_row = jnp.zeros((seqs_dev, 1, feat_width), jnp.float32)
    even_rows = jnp.concatenate([weight[0] * upstream, zero_row], 1) + jnp.concatenate(
        [zero_row, weight[2] * upstream], 1
    )
    odd_rows = jnp.concatenate([weight[1] * upstream, zero_row], 1) + jnp.concatenate(
        [zero_row, weight[3] * upstream], 1
    )
    spread = jnp.stack([even_rows, odd_rows], 2).reshape(seqs_dev, 2 * out_rows + 2, feat_width)
    weight_grad = jnp.stack(
        [
            jnp.sum(
                upstream * extended[:, offset : offset + 2 * out_rows : 2].astype(jnp.float32),
                (0, 1),
            )
            for offset in range(4)
        ]
    )
    return (spread, weight_grad)


def move_near(moved_rows, shift_by):
    return passed_along(moved_rows, "seq", shift_by)


def move_grads(moved_rows, shift_by):
    return passed_along(moved_rows.astype(jnp.bfloat16), "seq", shift_by).astype(moved_rows.dtype)


def per_device(queries, key_rows, value_rows, conv_key, conv_value, grad_out):
    seqs_dev, tok_rows, feat_width = queries.shape
    levels = conv_key.shape[0]
    head_count = HEADS
    head_size = HEAD_DIM
    blk_rows = BLOCK
    blocks_here = tok_rows // blk_rows
    local_top = blocks_here.bit_length() - 1
    seq_devices = lax.axis_size("seq")
    dev_index = lax.axis_index("seq")
    total_blocks = blocks_here * seq_devices
    score_scale = head_size ** (-0.5)
    pair_width = 2 * feat_width
    group_heads = 2
    kv_weight = jnp.stack(
        [
            conv_key.reshape(levels, 4, head_count, head_size),
            conv_value.reshape(levels, 4, head_count, head_size),
        ],
        3,
    ).reshape(levels, 4, pair_width)
    fine_pairs = jnp.stack(
        [
            key_rows.reshape(seqs_dev, tok_rows, head_count, head_size),
            value_rows.reshape(seqs_dev, tok_rows, head_count, head_size),
        ],
        3,
    ).reshape(seqs_dev, tok_rows, pair_width)
    own_rows = [fine_pairs]
    left_rims = [move_near(fine_pairs[:, -blk_rows:], 1)]
    right_rims = [move_near(fine_pairs[:, :blk_rows], -1)]
    extended_local = [None]
    level_id = 1
    extended = jnp.concatenate([left_rims[level_id - 1][:, -2:], own_rows[level_id - 1]], 1)
    extended_local.append(extended)
    coarse = coarsen(extended, kv_weight[level_id - 1])
    own_rows.append(coarse)
    left_rims.append(move_near(coarse, 1))
    right_rims.append(move_near(coarse, -1))
    block_now = own_rows[local_top]
    left_now = left_rims[local_top]
    group_lefts, group_rights, group_extended, group_first = ([], [], [], [])
    for level_id in range(local_top + 1, levels + 1):
        swap_bit = level_id - local_top - 1
        extended = jnp.concatenate([left_now[:, -2:], block_now], 1)
        group_extended.append(extended)
        own_half = coarsen(extended, kv_weight[level_id - 1])
        partner = partner_2(own_half, "seq", swap_bit)
        is_first = dev_index // 2**swap_bit % 2 == 0
        group_first.append(is_first)
        block_now = jnp.where(
            is_first,
            jnp.concatenate([own_half, partner], 1),
            jnp.concatenate([partner, own_half], 1),
        )
        stride_dev = 2 ** (level_id - local_top)
        left_now = move_near(block_now, stride_dev)
        right_now = move_near(block_now, -stride_dev)
        group_lefts.append(left_now)
        group_rights.append(right_now)
    glob_blocks = dev_index * blocks_here + jnp.arange(blocks_here, dtype=jnp.int32)
    always = jnp.ones((blocks_here,), jnp.bool_)
    sources = []
    pieces = []
    for level_id in range(local_top + 1):
        block_count = blocks_here >> level_id
        padded = jnp.concatenate([left_rims[level_id], own_rows[level_id], right_rims[level_id]], 1)
        sources.append(
            padded.reshape(seqs_dev, block_count + 2, blk_rows, head_count, 2, head_size)
        )
        coarse_id = glob_blocks // 2**level_id
        spread = 2**level_id
        pieces.append((level_id, 0, spread, coarse_id >= 1))
        if level_id == 0:
            pieces.append((0, 1, 1, always))
        pieces.append((level_id, 2, spread, coarse_id + 1 < total_blocks // 2**level_id))
    for slot_id in range(levels - local_top):
        level_id = local_top + 1 + slot_id
        coarse_id = glob_blocks // 2**level_id
        sources.append(
            group_lefts[slot_id].reshape(seqs_dev, 1, blk_rows, head_count, 2, head_size)
        )
        pieces.append((len(sources) - 1, 0, blocks_here, coarse_id >= 1))
        sources.append(
            group_rights[slot_id].reshape(seqs_dev, 1, blk_rows, head_count, 2, head_size)
        )
        pieces.append(
            (len(sources) - 1, 0, blocks_here, coarse_id + 1 < total_blocks // 2**level_id)
        )
    query_blocks = queries.reshape(seqs_dev, blocks_here, blk_rows, head_count, head_size)
    out_blocks = grad_out.reshape(seqs_dev, blocks_here, blk_rows, head_count, head_size)

    def head_group(group_id, loop_state):
        attended_acc, grad_q_acc, source_grads, log_totals, row_deltas = loop_state
        head_start = group_id * group_heads
        q_part = lax.dynamic_slice_in_dim(query_blocks, head_start, group_heads, 3)
        do_part = lax.dynamic_slice_in_dim(out_blocks, head_start, group_heads, 3)
        source_parts = [
            lax.dynamic_slice_in_dim(source, head_start, group_heads, 3) for source in sources
        ]
        score_list = []
        views = []
        for source_id, offset, spread, valid_mask in pieces:
            block_count = blocks_here // spread
            key_blocks = source_parts[source_id][:, offset : offset + block_count]
            q_view = q_part.reshape(seqs_dev, block_count, spread, blk_rows, group_heads, head_size)
            do_view = do_part.reshape(
                seqs_dev, block_count, spread, blk_rows, group_heads, head_size
            )
            raw_scores = jnp.einsum(
                "bnrqhe,bnkhe->bnrhqk",
                q_view,
                key_blocks[..., 0, :],
                preferred_element_type=jnp.float32,
            )
            raw_scores = (
                raw_scores.reshape(seqs_dev, blocks_here, group_heads, blk_rows, blk_rows)
                * score_scale
            )
            score_list.append(
                jnp.where(valid_mask[None, :, None, None, None], raw_scores, -jnp.inf)
            )
            views.append((key_blocks, q_view, do_view, block_count, spread))
        all_scores = jnp.concatenate(score_list, 4)
        row_max = jnp.max(all_scores, 4, keepdims=True)
        exp_scores = jnp.exp(all_scores - row_max)
        summed = jnp.sum(exp_scores, 4, keepdims=True)
        prob_full = exp_scores / summed
        probs_low = prob_full.astype(jnp.bfloat16)
        attended_part = jnp.zeros(
            (seqs_dev, blocks_here, blk_rows, group_heads, head_size), jnp.float32
        )
        grad_prob_list = []
        for piece_id, (key_blocks, q_view, do_view, block_count, spread) in enumerate(views):
            p_slice = probs_low[..., piece_id * blk_rows : (piece_id + 1) * blk_rows].reshape(
                seqs_dev, block_count, spread, group_heads, blk_rows, blk_rows
            )
            attended_part = attended_part + jnp.einsum(
                "bnrhqk,bnkhe->bnrqhe",
                p_slice,
                key_blocks[..., 1, :],
                preferred_element_type=jnp.float32,
            ).reshape(attended_part.shape)
            grad_prob = jnp.einsum(
                "bnrqhe,bnkhe->bnrhqk",
                do_view,
                key_blocks[..., 1, :],
                preferred_element_type=jnp.float32,
            )
            grad_prob_list.append(
                grad_prob.reshape(seqs_dev, blocks_here, group_heads, blk_rows, blk_rows)
            )
        grad_prob_all = jnp.concatenate(grad_prob_list, 4)
        row_delta = jnp.sum(prob_full * grad_prob_all, 4, keepdims=True)
        dscore = (prob_full * (grad_prob_all - row_delta) * score_scale).astype(jnp.bfloat16)
        grad_q_part = jnp.zeros(
            (seqs_dev, blocks_here, blk_rows, group_heads, head_size), jnp.float32
        )
        group_grads = [jnp.zeros(part_arr.shape, jnp.float32) for part_arr in source_parts]
        for piece_id, (key_blocks, q_view, do_view, block_count, spread) in enumerate(views):
            source_id, offset = (pieces[piece_id][0], pieces[piece_id][1])
            p_slice = probs_low[..., piece_id * blk_rows : (piece_id + 1) * blk_rows].reshape(
                seqs_dev, block_count, spread, group_heads, blk_rows, blk_rows
            )
            ds_slice = dscore[..., piece_id * blk_rows : (piece_id + 1) * blk_rows].reshape(
                seqs_dev, block_count, spread, group_heads, blk_rows, blk_rows
            )
            grad_q_part = grad_q_part + jnp.einsum(
                "bnrhqk,bnkhe->bnrqhe",
                ds_slice,
                key_blocks[..., 0, :],
                preferred_element_type=jnp.float32,
            ).reshape(grad_q_part.shape)
            key_grad = jnp.einsum(
                "bnrhqk,bnrqhe->bnkhe", ds_slice, q_view, preferred_element_type=jnp.float32
            )
            value_grad = jnp.einsum(
                "bnrhqk,bnrqhe->bnkhe", p_slice, do_view, preferred_element_type=jnp.float32
            )
            pair_grad = jnp.stack([key_grad, value_grad], 4)
            group_grads[source_id] = (
                group_grads[source_id].at[:, offset : offset + block_count].add(pair_grad)
            )
        attended_acc = lax.dynamic_update_slice_in_dim(
            attended_acc, attended_part.astype(jnp.bfloat16), head_start, 3
        )
        grad_q_acc = lax.dynamic_update_slice_in_dim(
            grad_q_acc, grad_q_part.astype(jnp.bfloat16), head_start, 3
        )
        source_grads = tuple(
            (
                lax.dynamic_update_slice_in_dim(whole, group_part, head_start, 3)
                for whole, group_part in zip(source_grads, group_grads)
            )
        )
        log_totals = lax.dynamic_update_slice_in_dim(
            log_totals, (row_max + jnp.log(summed))[..., 0], head_start, 2
        )
        row_deltas = lax.dynamic_update_slice_in_dim(row_deltas, row_delta[..., 0], head_start, 2)
        return (attended_acc, grad_q_acc, source_grads, log_totals, row_deltas)

    start_state = (
        jnp.zeros((seqs_dev, blocks_here, blk_rows, head_count, head_size), jnp.bfloat16),
        jnp.zeros((seqs_dev, blocks_here, blk_rows, head_count, head_size), jnp.bfloat16),
        tuple((jnp.zeros(source.shape, jnp.float32) for source in sources)),
        jnp.zeros((seqs_dev, blocks_here, head_count, blk_rows), jnp.float32),
        jnp.zeros((seqs_dev, blocks_here, head_count, blk_rows), jnp.float32),
    )
    attended_acc, grad_q_acc, source_grads, log_totals, row_deltas = lax.fori_loop(
        0, head_count // group_heads, head_group, start_state
    )
    attended = attended_acc.reshape(seqs_dev, tok_rows, feat_width)
    grad_query = grad_q_acc.reshape(seqs_dev, tok_rows, feat_width)
    grad_left, grad_own, grad_right = ([], [], [])
    for level_id in range(local_top + 1):
        flat_grad = source_grads[level_id].reshape(seqs_dev, -1, pair_width)
        grad_left.append(flat_grad[:, :blk_rows])
        grad_own.append(flat_grad[:, blk_rows:-blk_rows])
        grad_right.append(flat_grad[:, -blk_rows:])
    group_left_grads = [
        source_grads[local_top + 1 + 2 * slot_id].reshape(seqs_dev, blk_rows, pair_width)
        for slot_id in range(levels - local_top)
    ]
    group_right_grads = [
        source_grads[local_top + 2 + 2 * slot_id].reshape(seqs_dev, blk_rows, pair_width)
        for slot_id in range(levels - local_top)
    ]
    weight_grads = [None] * levels
    carry_block = jnp.zeros((seqs_dev, blk_rows, pair_width), jnp.float32)
    carry_left = jnp.zeros((seqs_dev, 2, pair_width), jnp.float32)
    for level_id in range(levels, local_top, -1):
        slot_id = level_id - local_top - 1
        stride_dev = 2 ** (level_id - local_top)
        left_total = group_left_grads[slot_id].at[:, -2:].add(carry_left)
        block_total = (
            carry_block
            + move_grads(left_total, -stride_dev)
            + move_grads(group_right_grads[slot_id], stride_dev)
        )
        first_part = block_total[:, : blk_rows // 2]
        second_part = block_total[:, blk_rows // 2 :]
        keep_part = jnp.where(group_first[slot_id], first_part, second_part)
        give_part = jnp.where(group_first[slot_id], second_part, first_part)
        half_grad = keep_part + partner_2(give_part.astype(jnp.bfloat16), "seq", slot_id).astype(
            give_part.dtype
        )
        spread, weight_grads[level_id - 1] = coarsen_back(
            half_grad, group_extended[slot_id], kv_weight[level_id - 1]
        )
        carry_left = spread[:, :2]
        carry_block = spread[:, 2:]
    grad_left[local_top] = grad_left[local_top].at[:, -2:].add(carry_left)
    grad_own[local_top] = grad_own[local_top] + carry_block
    fine_left_conv = jnp.zeros((seqs_dev, blk_rows, pair_width), jnp.float32)
    level_id = 1
    from_right = move_grads(grad_left[level_id], -1)
    from_left = move_grads(grad_right[level_id], 1)
    level_grad = (
        grad_own[level_id].at[:, :blk_rows].add(from_left).at[:, -blk_rows:].add(from_right)
    )
    spread, weight_grads[level_id - 1] = coarsen_back(
        level_grad, extended_local[level_id], kv_weight[level_id - 1]
    )
    fine_left_conv = fine_left_conv.at[:, -2:].add(spread[:, :2])
    grad_own[level_id - 1] = grad_own[level_id - 1] + spread[:, 2:]

    def owner_terms(sent_rows, sent_stats, pair_rows):
        q_rows = sent_rows[:, :, :feat_width].reshape(seqs_dev, blk_rows, head_count, head_size)
        do_rows = sent_rows[:, :, feat_width:].reshape(seqs_dev, blk_rows, head_count, head_size)
        pair_view = pair_rows.reshape(seqs_dev, blk_rows, head_count, 2, head_size)
        raw_scores = (
            jnp.einsum(
                "bqhe,bkhe->bhqk", q_rows, pair_view[..., 0, :], preferred_element_type=jnp.float32
            )
            * score_scale
        )
        prob_full = jnp.exp(raw_scores - sent_stats[:, 0][..., None])
        grad_prob = jnp.einsum(
            "bqhe,bkhe->bhqk", do_rows, pair_view[..., 1, :], preferred_element_type=jnp.float32
        )
        dscore = (prob_full * (grad_prob - sent_stats[:, 1][..., None]) * score_scale).astype(
            jnp.bfloat16
        )
        key_grad = jnp.einsum("bhqk,bqhe->bkhe", dscore, q_rows, preferred_element_type=jnp.float32)
        value_grad = jnp.einsum(
            "bhqk,bqhe->bkhe",
            prob_full.astype(jnp.bfloat16),
            do_rows,
            preferred_element_type=jnp.float32,
        )
        return jnp.stack([key_grad, value_grad], 3).reshape(seqs_dev, blk_rows, pair_width)

    from_right = move_grads(fine_left_conv, -1)
    query_tail = jnp.concatenate([queries[:, -blk_rows:], grad_out[:, -blk_rows:]], 2)
    query_front = jnp.concatenate([queries[:, :blk_rows], grad_out[:, :blk_rows]], 2)
    stats_tail = jnp.stack([log_totals[:, -1], row_deltas[:, -1]], 1)
    stats_front = jnp.stack([log_totals[:, 0], row_deltas[:, 0]], 1)
    tail_from_left = move_near(query_tail, 1)
    front_from_right = move_near(query_front, -1)
    stats_from_left = move_grads(stats_tail, 1)
    stats_from_right = move_grads(stats_front, -1)
    left_terms = owner_terms(tail_from_left, stats_from_left, fine_pairs[:, :blk_rows])
    right_terms = owner_terms(front_from_right, stats_from_right, fine_pairs[:, -blk_rows:])
    fine_grad = (
        grad_own[0].at[:, :blk_rows].add(left_terms).at[:, -blk_rows:].add(right_terms + from_right)
    )
    grad_pairs = fine_grad.reshape(seqs_dev, tok_rows, head_count, 2, head_size)
    grad_key = (
        grad_pairs[:, :, :, 0, :].reshape(seqs_dev, tok_rows, feat_width).astype(jnp.bfloat16)
    )
    grad_value = (
        grad_pairs[:, :, :, 1, :].reshape(seqs_dev, tok_rows, feat_width).astype(jnp.bfloat16)
    )
    weight_sum = lax.psum(jnp.stack(weight_grads), ("seq", "dp")).reshape(
        levels, 4, head_count, 2, head_size
    )
    grad_conv_key = weight_sum[:, :, :, 0, :].reshape(levels, 4, feat_width)
    grad_conv_value = weight_sum[:, :, :, 1, :].reshape(levels, 4, feat_width)
    return (attended, grad_query, grad_key, grad_value, grad_conv_key, grad_conv_value)


LOG2E = 1.4426950408889634
MASKED = -1e30


def level_bases(blocks, levels):
    bases, offset = [], 0
    for level_id in range(levels + 1):
        bases.append(offset)
        offset += (blocks >> level_id) + 2
    return bases, offset


def build_levels(take_rows, weight, bases, blocks, levels, wide_ref, low_ref, turned_ref):
    zero_wide = jnp.zeros((BLOCK, HEAD_DIM), jnp.float32)
    zero_low = jnp.zeros((BLOCK, HEAD_DIM), jnp.bfloat16)
    for level_id in range(levels + 1):
        for pad in (bases[level_id], bases[level_id] + (blocks >> level_id) + 1):
            wide_ref[pad * BLOCK : (pad + 1) * BLOCK] = zero_wide
            low_ref[pad] = zero_low
            turned_ref[pad] = zero_low

    def put(index, low):
        wide = low.astype(jnp.float32)
        wide_ref[pl.ds(pl.multiple_of(index * BLOCK, BLOCK), BLOCK)] = wide
        low_ref[index] = low
        turned_ref[index] = wide.T.astype(jnp.bfloat16)

    def put_pair(distance, carry):
        pair, rows = take_rows(distance)
        put(1 + 2 * pair, rows[:BLOCK])
        put(2 + 2 * pair, rows[BLOCK:])
        return carry

    lax.fori_loop(0, blocks // 2, put_pair, 0)
    for level_id in range(1, levels + 1):
        for block in range(blocks >> level_id):
            start = (bases[level_id - 1] + 1 + 2 * block) * BLOCK - 2
            summed = jnp.zeros((BLOCK, HEAD_DIM), jnp.float32)
            for tap in range(4):
                row = 4 * (level_id - 1) + tap
                summed = summed + weight(row) * wide_ref[pl.ds(start + tap, BLOCK, stride=2)]
            put(bases[level_id] + 1 + block, summed.astype(jnp.bfloat16))


def attend_pair(pair, q_rows, do_rows, bases, blocks, levels, keys, values, scratch):
    key_low, key_turned, key_grad = keys
    value_low, value_turned, value_grad = values
    score_ref, dprob_ref = scratch
    scale = HEAD_DIM**-0.5
    two = 2 * BLOCK
    q_turned = q_rows.astype(jnp.float32).T.astype(jnp.bfloat16)
    do_turned = do_rows.astype(jnp.float32).T.astype(jnp.bfloat16)
    lane = lax.broadcasted_iota(jnp.int32, (1, two), 1)
    pairs = blocks // 2
    places = [2 * pair, 2 * pair + 1, 2 * pair + 2, 2 * pair + 3]
    spans = [
        (0, jnp.where(pair > 0, BLOCK, 0)),
        None,
        None,
        (jnp.where(pair + 1 < pairs, BLOCK, two), two),
    ]
    for level_id in range(1, levels + 1):
        coarse_id = pair // 2 ** (level_id - 1)
        places += [bases[level_id] + coarse_id, bases[level_id] + coarse_id + 2]
        spans += [
            (0, jnp.where(coarse_id >= 1, two, 0)),
            (0, jnp.where(coarse_id + 1 < blocks >> level_id, two, 0)),
        ]
    row_max = jnp.full((1, two), MASKED, jnp.float32)
    for piece, place in enumerate(places):
        score = jnp.dot(key_low[place], q_turned, preferred_element_type=jnp.float32)
        if spans[piece] is not None:
            first, last = spans[piece]
            score = jnp.where((lane >= first) & (lane < last), score, MASKED)
        score_ref[piece] = score
        row_max = jnp.maximum(row_max, jnp.max(score, 0, keepdims=True))
    total = jnp.zeros((1, two), jnp.float32)
    weighted = jnp.zeros((1, two), jnp.float32)
    for piece, place in enumerate(places):
        raised = jnp.exp2((score_ref[piece] - row_max) * (scale * LOG2E))
        dprob = jnp.dot(value_low[place], do_turned, preferred_element_type=jnp.float32)
        score_ref[piece] = raised
        dprob_ref[piece] = dprob
        total = total + jnp.sum(raised, 0, keepdims=True)
        weighted = weighted + jnp.sum(raised * dprob, 0, keepdims=True)
    inverse = 1.0 / total
    delta = weighted * inverse
    attended = jnp.zeros((HEAD_DIM, two), jnp.float32)
    grad_q = jnp.zeros((HEAD_DIM, two), jnp.float32)
    for piece in range(0, len(places), 2):
        lows, dlows = [], []
        for step in (piece, piece + 1):
            rows = pl.ds(pl.multiple_of(places[step] * BLOCK, BLOCK), BLOCK)
            probs = score_ref[step] * inverse
            probs_low = probs.astype(jnp.bfloat16)
            dscore = (probs * (dprob_ref[step] - delta)).astype(jnp.bfloat16)
            value_grad[rows] += jnp.dot(probs_low, do_rows, preferred_element_type=jnp.float32)
            key_grad[rows] += jnp.dot(dscore, q_rows, preferred_element_type=jnp.float32)
            lows.append(probs_low)
            dlows.append(dscore)
        here, there = places[piece], places[piece + 1]
        value_two = jnp.concatenate([value_turned[here], value_turned[there]], 1)
        key_two = jnp.concatenate([key_turned[here], key_turned[there]], 1)
        attended = attended + jnp.dot(
            value_two, jnp.concatenate(lows, 0), preferred_element_type=jnp.float32
        )
        grad_q = grad_q + jnp.dot(
            key_two, jnp.concatenate(dlows, 0), preferred_element_type=jnp.float32
        )
    return attended.T.astype(jnp.bfloat16), (grad_q * scale).T.astype(jnp.bfloat16)


def coarsen_gradients(weight, bases, blocks, levels, wide_ref, grad_ref, put_weight_grad):
    for level_id in range(levels, 0, -1):
        tap_sums = [jnp.zeros((1, HEAD_DIM), jnp.float32) for _ in range(4)]
        for block in range(blocks >> level_id):
            start = (bases[level_id] + 1 + block) * BLOCK
            upstream = grad_ref[start : start + BLOCK]
            following = grad_ref[start + 1 : start + 1 + BLOCK]
            below = (bases[level_id - 1] + 1 + 2 * block) * BLOCK
            taps = [weight(4 * (level_id - 1) + tap) for tap in range(4)]
            grad_ref[pl.ds(below, BLOCK, stride=2)] += taps[2] * upstream + taps[0] * following
            grad_ref[pl.ds(below + 1, BLOCK, stride=2)] += taps[3] * upstream + taps[1] * following
            for tap in range(4):
                tap_sums[tap] = tap_sums[tap] + jnp.sum(
                    upstream * wide_ref[pl.ds(below - 2 + tap, BLOCK, stride=2)], 0, keepdims=True
                )
        for tap in range(4):
            put_weight_grad(4 * (level_id - 1) + tap, tap_sums[tap])


def columns(head):
    return pl.ds(pl.multiple_of(head * HEAD_DIM, HEAD_DIM), HEAD_DIM)


def head_kernel(
    levels,
    ring,
    groups,
    q_hbm,
    key_hbm,
    value_hbm,
    do_hbm,
    conv_key_ref,
    conv_value_ref,
    att_hbm,
    grad_q_hbm,
    grad_key_hbm,
    grad_value_hbm,
    conv_key_grad,
    conv_value_grad,
    rows_ref,
    out_ref,
    conv_here,
    conv_parts,
    conv_total,
    key_wide,
    key_low,
    key_turned,
    key_grad,
    value_wide,
    value_low,
    value_turned,
    value_grad,
    score_ref,
    dprob_ref,
    in_send,
    in_recv,
    out_send,
    out_recv,
    part_send,
    part_recv,
    total_send,
    total_recv,
):
    me = lax.axis_index("seq")
    group = lax.axis_index("dp")
    blocks = 2 * ring
    bases, _ = level_bases(blocks, levels)
    scale = HEAD_DIM**-0.5
    sources = (q_hbm, key_hbm, value_hbm, do_hbm)
    conv_grads = (conv_key_grad, conv_value_grad)
    results = (att_hbm, grad_q_hbm, grad_key_hbm, grad_value_hbm)

    def after(distance):
        return lax.rem(me + distance, ring)

    def before(distance):
        return lax.rem(me + ring - distance, ring)

    barrier = pltpu.get_barrier_semaphore()
    for distance in range(1, ring):
        pl.semaphore_signal(
            barrier,
            inc=1,
            device_id={"seq": after(distance)},
            device_id_type=pl.DeviceIdType.MESH,
        )
    for distance in range(1, groups):
        pl.semaphore_signal(
            barrier,
            inc=1,
            device_id={"dp": lax.rem(group + distance, groups)},
            device_id_type=pl.DeviceIdType.MESH,
        )
    pl.semaphore_wait(barrier, ring + groups - 2)

    def inbound(array, distance, landing):
        return pltpu.make_async_remote_copy(
            src_ref=sources[array].at[0, :, columns(after(distance))],
            dst_ref=rows_ref.at[landing, array],
            send_sem=in_send.at[array, distance],
            recv_sem=in_recv.at[array, distance],
            device_id={"seq": after(distance)},
            device_id_type=pl.DeviceIdType.MESH,
        )

    def inbound_own(array):
        return pltpu.make_async_copy(
            sources[array].at[0, :, columns(me)], rows_ref.at[me, array], in_recv.at[array, 0]
        )

    def outbound(array, distance, origin):
        return pltpu.make_async_remote_copy(
            src_ref=out_ref.at[before(distance), array],
            dst_ref=results[array].at[0, :, columns(origin)],
            send_sem=out_send.at[array, distance],
            recv_sem=out_recv.at[array, distance],
            device_id={"seq": before(distance)},
            device_id_type=pl.DeviceIdType.MESH,
        )

    def outbound_own(array):
        return pltpu.make_async_copy(
            out_ref.at[me, array], results[array].at[0, :, columns(me)], out_recv.at[array, 0]
        )

    def send(*arrays):
        for array in arrays:
            inbound_own(array).start()

        def step(distance, carry):
            for array in arrays:
                inbound(array, distance, me).start()
            return carry

        lax.fori_loop(1, ring, step, 0)

    send(1)
    send(2)
    conv_here[0] = conv_key_ref[:, :, columns(me)]
    conv_here[1] = conv_value_ref[:, :, columns(me)]

    def arrived(array, distance):
        @pl.when(distance == 0)
        def _():
            inbound_own(array).wait()

        @pl.when(distance > 0)
        def _():
            inbound(array, distance, before(distance)).wait_recv()

    def leave(array, distance):
        @pl.when(distance == 0)
        def _():
            outbound_own(array).start()

        @pl.when(distance > 0)
        def _():
            outbound(array, distance, me).start()

    def taker(array):
        def take_rows(distance):
            arrived(array, distance)
            return before(distance), rows_ref[before(distance), array]

        return take_rows

    def key_weight(row):
        return conv_here[0, row // 4, row % 4 : row % 4 + 1]

    def value_weight(row):
        return conv_here[1, row // 4, row % 4 : row % 4 + 1]

    shape = (bases, blocks, levels)
    key_grad[...] = jnp.zeros_like(key_grad)
    value_grad[...] = jnp.zeros_like(value_grad)
    build_levels(taker(1), key_weight, *shape, key_wide, key_low, key_turned)
    send(0, 3)
    build_levels(taker(2), value_weight, *shape, value_wide, value_low, value_turned)

    def step(distance, carry):
        pair = before(distance)
        arrived(0, distance)
        arrived(3, distance)
        attended, grad_q = attend_pair(
            pair,
            rows_ref[pair, 0],
            rows_ref[pair, 3],
            *shape,
            (key_low, key_turned, key_grad),
            (value_low, value_turned, value_grad),
            (score_ref, dprob_ref),
        )
        out_ref[pair, 0] = attended
        out_ref[pair, 1] = grad_q
        leave(0, distance)
        leave(1, distance)
        return carry

    lax.fori_loop(0, ring, step, 0)

    def put_key(row, value):
        conv_total[0, row // 4, row % 4 : row % 4 + 1] = value * scale

    def put_value(row, value):
        conv_total[1, row // 4, row % 4 : row % 4 + 1] = value

    def finisher(array, grad_ref, factor):
        def finish(distance, carry):
            pair = before(distance)
            rows = pl.ds(pl.multiple_of((1 + 2 * pair) * BLOCK, BLOCK), 2 * BLOCK)
            out_ref[pair, array] = (grad_ref[rows] * factor).astype(jnp.bfloat16)
            leave(array, distance)
            return carry

        return finish

    coarsen_gradients(key_weight, *shape, key_wide, key_grad, put_key)
    lax.fori_loop(0, ring, finisher(2, key_grad, scale), 0)
    coarsen_gradients(value_weight, *shape, value_wide, value_grad, put_value)

    def part(distance, slot):
        other = lax.rem(group + distance, groups)
        return pltpu.make_async_remote_copy(
            src_ref=conv_parts.at[group],
            dst_ref=conv_parts.at[slot],
            send_sem=part_send.at[distance],
            recv_sem=part_recv.at[distance],
            device_id={"dp": other},
            device_id_type=pl.DeviceIdType.MESH,
        )

    def gathered(kind, distance, head):
        return pltpu.make_async_remote_copy(
            src_ref=conv_total.at[kind],
            dst_ref=conv_grads[kind].at[:, :, columns(head)],
            send_sem=total_send.at[kind, distance],
            recv_sem=total_recv.at[kind, distance],
            device_id={"seq": after(distance)},
            device_id_type=pl.DeviceIdType.MESH,
        )

    conv_parts[group] = conv_total[...]
    for distance in range(1, groups):
        part(distance, group).start()
    lax.fori_loop(0, ring, finisher(3, value_grad, 1.0), 0)
    for distance in range(1, groups):
        part(distance, lax.rem(group + groups - distance, groups)).wait_recv()
    conv_sum = conv_parts[0]
    for slot in range(1, groups):
        conv_sum = conv_sum + conv_parts[slot]
    conv_total[...] = conv_sum
    for kind in range(2):
        conv_grads[kind][:, :, columns(me)] = conv_sum[kind]
        for distance in range(1, ring):
            gathered(kind, distance, me).start()

    for array in range(4):
        outbound_own(array).wait()

    def settle(distance, carry):
        for array in range(4):
            inbound(array, distance, me).wait_send()
            outbound(array, distance, me).wait_send()
            outbound(array, distance, after(distance)).wait_recv()
        for kind in range(2):
            gathered(kind, distance, me).wait_send()
            gathered(kind, distance, before(distance)).wait_recv()
        return carry

    lax.fori_loop(1, ring, settle, 0)
    for distance in range(1, groups):
        part(distance, group).wait_send()


def stack_scratch(blocks, levels):
    total = level_bases(blocks, levels)[1]
    flat = pltpu.VMEM((total * BLOCK, HEAD_DIM), jnp.float32)
    low = pltpu.VMEM((total, BLOCK, HEAD_DIM), jnp.bfloat16)
    return [flat, low, low, flat]


def per_device_heads(queries, key_rows, value_rows, conv_key, conv_value, grad_out):
    tok_rows = queries.shape[1]
    levels = conv_key.shape[0]
    ring, groups = lax.axis_size("seq"), lax.axis_size("dp")
    like = jax.ShapeDtypeStruct(queries.shape, jnp.bfloat16)
    conv_like = jax.ShapeDtypeStruct(conv_key.shape, jnp.float32)
    scores = pltpu.VMEM((4 + 2 * levels, BLOCK, 2 * BLOCK), jnp.float32)
    rows = pltpu.VMEM((ring, 4, tok_rows, HEAD_DIM), jnp.bfloat16)
    small = (2, levels, 4, HEAD_DIM)
    dma = pltpu.SemaphoreType.DMA
    in_hbm = pl.BlockSpec(memory_space=pltpu.HBM)
    in_vmem = pl.BlockSpec(memory_space=pltpu.VMEM)
    return pl.pallas_call(
        functools.partial(head_kernel, levels, ring, groups),
        out_shape=(like, like, like, like, conv_like, conv_like),
        in_specs=[in_hbm] * 4 + [in_vmem] * 2,
        out_specs=[in_hbm] * 4 + [in_vmem] * 2,
        scratch_shapes=[
            rows,
            rows,
            pltpu.VMEM(small, jnp.float32),
            pltpu.VMEM((groups,) + small, jnp.float32),
            pltpu.VMEM(small, jnp.float32),
        ]
        + stack_scratch(2 * ring, levels) * 2
        + [scores, scores]
        + [dma((4, ring))] * 4
        + [dma((groups,))] * 2
        + [dma((2, ring))] * 2,
        compiler_params=pltpu.CompilerParams(
            collective_id=0, has_side_effects=True, vmem_limit_bytes=56 * 2**20
        ),
    )(queries, key_rows, value_rows, grad_out, conv_key, conv_value)


def solution(mesh):
    in_specs = (
        P("dp", "seq", None),
        P("dp", "seq", None),
        P("dp", "seq", None),
        P(),
        P(),
        P("dp", "seq", None),
    )
    out_specs = (
        P("dp", "seq", None),
        P("dp", "seq", None),
        P("dp", "seq", None),
        P("dp", "seq", None),
        P(),
        P(),
    )
    def chosen(*args):
        seq_devices = lax.axis_size("seq")
        fits = seq_devices == HEADS and args[0].shape[:2] == (1, 2 * BLOCK)
        return (per_device_heads if fits else per_device)(*args)

    return jax.shard_map(
        chosen, mesh=mesh, in_specs=in_specs, out_specs=out_specs, check_vma=False
    )
```

```python
import functools

import jax
import jax.numpy as jnp
from jax import lax
from jax.experimental import pallas as pl
from jax.experimental.pallas import tpu as pltpu
from jax.sharding import PartitionSpec as P

HEADS = 8
HEAD_DIM = 128
BLOCK = 128


def passed_along(value, axis, steps):
    count = lax.axis_size(axis)
    initial, last = (max(0, -steps), min(count, count - steps))
    return lax.ppermute(value, axis, [(source, source + steps) for source in range(initial, last)])


def partner_2(array, axis, distance):
    return lax.ppermute(array, axis, [(i, i ^ 1 << distance) for i in range(lax.axis_size(axis))])


def coarsen(extended, weight):
    out_rows = (extended.shape[1] - 2) // 2
    summed = weight[0] * extended[:, 0 : 2 * out_rows : 2].astype(jnp.float32)
    for offset in range(1, 4):
        summed = summed + weight[offset] * extended[:, offset : offset + 2 * out_rows : 2].astype(
            jnp.float32
        )
    return summed.astype(jnp.bfloat16)


def coarsen_back(upstream, extended, weight):
    seqs_dev, out_rows, feat_width = upstream.shape
    zero_row = jnp.zeros((seqs_dev, 1, feat_width), jnp.float32)
    even_rows = jnp.concatenate([weight[0] * upstream, zero_row], 1) + jnp.concatenate(
        [zero_row, weight[2] * upstream], 1
    )
    odd_rows = jnp.concatenate([weight[1] * upstream, zero_row], 1) + jnp.concatenate(
        [zero_row, weight[3] * upstream], 1
    )
    spread = jnp.stack([even_rows, odd_rows], 2).reshape(seqs_dev, 2 * out_rows + 2, feat_width)
    weight_grad = jnp.stack(
        [
            jnp.sum(
                upstream * extended[:, offset : offset + 2 * out_rows : 2].astype(jnp.float32),
                (0, 1),
            )
            for offset in range(4)
        ]
    )
    return (spread, weight_grad)


def move_near(moved_rows, shift_by):
    return passed_along(moved_rows, "seq", shift_by)


def move_grads(moved_rows, shift_by):
    return passed_along(moved_rows.astype(jnp.bfloat16), "seq", shift_by).astype(moved_rows.dtype)


def per_device(queries, key_rows, value_rows, conv_key, conv_value, grad_out):
    seqs_dev, tok_rows, feat_width = queries.shape
    levels = conv_key.shape[0]
    head_count = HEADS
    head_size = HEAD_DIM
    blk_rows = BLOCK
    blocks_here = tok_rows // blk_rows
    local_top = blocks_here.bit_length() - 1
    seq_devices = lax.axis_size("seq")
    dev_index = lax.axis_index("seq")
    total_blocks = blocks_here * seq_devices
    score_scale = head_size ** (-0.5)
    pair_width = 2 * feat_width
    group_heads = 2
    kv_weight = jnp.stack(
        [
            conv_key.reshape(levels, 4, head_count, head_size),
            conv_value.reshape(levels, 4, head_count, head_size),
        ],
        3,
    ).reshape(levels, 4, pair_width)
    fine_pairs = jnp.stack(
        [
            key_rows.reshape(seqs_dev, tok_rows, head_count, head_size),
            value_rows.reshape(seqs_dev, tok_rows, head_count, head_size),
        ],
        3,
    ).reshape(seqs_dev, tok_rows, pair_width)
    own_rows = [fine_pairs]
    left_rims = [move_near(fine_pairs[:, -blk_rows:], 1)]
    right_rims = [move_near(fine_pairs[:, :blk_rows], -1)]
    extended_local = [None]
    level_id = 1
    extended = jnp.concatenate([left_rims[level_id - 1][:, -2:], own_rows[level_id - 1]], 1)
    extended_local.append(extended)
    coarse = coarsen(extended, kv_weight[level_id - 1])
    own_rows.append(coarse)
    left_rims.append(move_near(coarse, 1))
    right_rims.append(move_near(coarse, -1))
    block_now = own_rows[local_top]
    left_now = left_rims[local_top]
    group_lefts, group_rights, group_extended, group_first = ([], [], [], [])
    for level_id in range(local_top + 1, levels + 1):
        swap_bit = level_id - local_top - 1
        extended = jnp.concatenate([left_now[:, -2:], block_now], 1)
        group_extended.append(extended)
        own_half = coarsen(extended, kv_weight[level_id - 1])
        partner = partner_2(own_half, "seq", swap_bit)
        is_first = dev_index // 2**swap_bit % 2 == 0
        group_first.append(is_first)
        block_now = jnp.where(
            is_first,
            jnp.concatenate([own_half, partner], 1),
            jnp.concatenate([partner, own_half], 1),
        )
        stride_dev = 2 ** (level_id - local_top)
        left_now = move_near(block_now, stride_dev)
        right_now = move_near(block_now, -stride_dev)
        group_lefts.append(left_now)
        group_rights.append(right_now)
    glob_blocks = dev_index * blocks_here + jnp.arange(blocks_here, dtype=jnp.int32)
    always = jnp.ones((blocks_here,), jnp.bool_)
    sources = []
    pieces = []
    for level_id in range(local_top + 1):
        block_count = blocks_here >> level_id
        padded = jnp.concatenate([left_rims[level_id], own_rows[level_id], right_rims[level_id]], 1)
        sources.append(
            padded.reshape(seqs_dev, block_count + 2, blk_rows, head_count, 2, head_size)
        )
        coarse_id = glob_blocks // 2**level_id
        spread = 2**level_id
        pieces.append((level_id, 0, spread, coarse_id >= 1))
        if level_id == 0:
            pieces.append((0, 1, 1, always))
        pieces.append((level_id, 2, spread, coarse_id + 1 < total_blocks // 2**level_id))
    for slot_id in range(levels - local_top):
        level_id = local_top + 1 + slot_id
        coarse_id = glob_blocks // 2**level_id
        sources.append(
            group_lefts[slot_id].reshape(seqs_dev, 1, blk_rows, head_count, 2, head_size)
        )
        pieces.append((len(sources) - 1, 0, blocks_here, coarse_id >= 1))
        sources.append(
            group_rights[slot_id].reshape(seqs_dev, 1, blk_rows, head_count, 2, head_size)
        )
        pieces.append(
            (len(sources) - 1, 0, blocks_here, coarse_id + 1 < total_blocks // 2**level_id)
        )
    query_blocks = queries.reshape(seqs_dev, blocks_here, blk_rows, head_count, head_size)
    out_blocks = grad_out.reshape(seqs_dev, blocks_here, blk_rows, head_count, head_size)

    def head_group(group_id, loop_state):
        attended_acc, grad_q_acc, source_grads, log_totals, row_deltas = loop_state
        head_start = group_id * group_heads
        q_part = lax.dynamic_slice_in_dim(query_blocks, head_start, group_heads, 3)
        do_part = lax.dynamic_slice_in_dim(out_blocks, head_start, group_heads, 3)
        source_parts = [
            lax.dynamic_slice_in_dim(source, head_start, group_heads, 3) for source in sources
        ]
        score_list = []
        views = []
        for source_id, offset, spread, valid_mask in pieces:
            block_count = blocks_here // spread
            key_blocks = source_parts[source_id][:, offset : offset + block_count]
            q_view = q_part.reshape(seqs_dev, block_count, spread, blk_rows, group_heads, head_size)
            do_view = do_part.reshape(
                seqs_dev, block_count, spread, blk_rows, group_heads, head_size
            )
            raw_scores = jnp.einsum(
                "bnrqhe,bnkhe->bnrhqk",
                q_view,
                key_blocks[..., 0, :],
                preferred_element_type=jnp.float32,
            )
            raw_scores = (
                raw_scores.reshape(seqs_dev, blocks_here, group_heads, blk_rows, blk_rows)
                * score_scale
            )
            score_list.append(
                jnp.where(valid_mask[None, :, None, None, None], raw_scores, -jnp.inf)
            )
            views.append((key_blocks, q_view, do_view, block_count, spread))
        all_scores = jnp.concatenate(score_list, 4)
        row_max = jnp.max(all_scores, 4, keepdims=True)
        exp_scores = jnp.exp(all_scores - row_max)
        summed = jnp.sum(exp_scores, 4, keepdims=True)
        prob_full = exp_scores / summed
        probs_low = prob_full.astype(jnp.bfloat16)
        attended_part = jnp.zeros(
            (seqs_dev, blocks_here, blk_rows, group_heads, head_size), jnp.float32
        )
        grad_prob_list = []
        for piece_id, (key_blocks, q_view, do_view, block_count, spread) in enumerate(views):
            p_slice = probs_low[..., piece_id * blk_rows : (piece_id + 1) * blk_rows].reshape(
                seqs_dev, block_count, spread, group_heads, blk_rows, blk_rows
            )
            attended_part = attended_part + jnp.einsum(
                "bnrhqk,bnkhe->bnrqhe",
                p_slice,
                key_blocks[..., 1, :],
                preferred_element_type=jnp.float32,
            ).reshape(attended_part.shape)
            grad_prob = jnp.einsum(
                "bnrqhe,bnkhe->bnrhqk",
                do_view,
                key_blocks[..., 1, :],
                preferred_element_type=jnp.float32,
            )
            grad_prob_list.append(
                grad_prob.reshape(seqs_dev, blocks_here, group_heads, blk_rows, blk_rows)
            )
        grad_prob_all = jnp.concatenate(grad_prob_list, 4)
        row_delta = jnp.sum(prob_full * grad_prob_all, 4, keepdims=True)
        dscore = (prob_full * (grad_prob_all - row_delta) * score_scale).astype(jnp.bfloat16)
        grad_q_part = jnp.zeros(
            (seqs_dev, blocks_here, blk_rows, group_heads, head_size), jnp.float32
        )
        group_grads = [jnp.zeros(part_arr.shape, jnp.float32) for part_arr in source_parts]
        for piece_id, (key_blocks, q_view, do_view, block_count, spread) in enumerate(views):
            source_id, offset = (pieces[piece_id][0], pieces[piece_id][1])
            p_slice = probs_low[..., piece_id * blk_rows : (piece_id + 1) * blk_rows].reshape(
                seqs_dev, block_count, spread, group_heads, blk_rows, blk_rows
            )
            ds_slice = dscore[..., piece_id * blk_rows : (piece_id + 1) * blk_rows].reshape(
                seqs_dev, block_count, spread, group_heads, blk_rows, blk_rows
            )
            grad_q_part = grad_q_part + jnp.einsum(
                "bnrhqk,bnkhe->bnrqhe",
                ds_slice,
                key_blocks[..., 0, :],
                preferred_element_type=jnp.float32,
            ).reshape(grad_q_part.shape)
            key_grad = jnp.einsum(
                "bnrhqk,bnrqhe->bnkhe", ds_slice, q_view, preferred_element_type=jnp.float32
            )
            value_grad = jnp.einsum(
                "bnrhqk,bnrqhe->bnkhe", p_slice, do_view, preferred_element_type=jnp.float32
            )
            pair_grad = jnp.stack([key_grad, value_grad], 4)
            group_grads[source_id] = (
                group_grads[source_id].at[:, offset : offset + block_count].add(pair_grad)
            )
        attended_acc = lax.dynamic_update_slice_in_dim(
            attended_acc, attended_part.astype(jnp.bfloat16), head_start, 3
        )
        grad_q_acc = lax.dynamic_update_slice_in_dim(
            grad_q_acc, grad_q_part.astype(jnp.bfloat16), head_start, 3
        )
        source_grads = tuple(
            (
                lax.dynamic_update_slice_in_dim(whole, group_part, head_start, 3)
                for whole, group_part in zip(source_grads, group_grads)
            )
        )
        log_totals = lax.dynamic_update_slice_in_dim(
            log_totals, (row_max + jnp.log(summed))[..., 0], head_start, 2
        )
        row_deltas = lax.dynamic_update_slice_in_dim(row_deltas, row_delta[..., 0], head_start, 2)
        return (attended_acc, grad_q_acc, source_grads, log_totals, row_deltas)

    start_state = (
        jnp.zeros((seqs_dev, blocks_here, blk_rows, head_count, head_size), jnp.bfloat16),
        jnp.zeros((seqs_dev, blocks_here, blk_rows, head_count, head_size), jnp.bfloat16),
        tuple((jnp.zeros(source.shape, jnp.float32) for source in sources)),
        jnp.zeros((seqs_dev, blocks_here, head_count, blk_rows), jnp.float32),
        jnp.zeros((seqs_dev, blocks_here, head_count, blk_rows), jnp.float32),
    )
    attended_acc, grad_q_acc, source_grads, log_totals, row_deltas = lax.fori_loop(
        0, head_count // group_heads, head_group, start_state
    )
    attended = attended_acc.reshape(seqs_dev, tok_rows, feat_width)
    grad_query = grad_q_acc.reshape(seqs_dev, tok_rows, feat_width)
    grad_left, grad_own, grad_right = ([], [], [])
    for level_id in range(local_top + 1):
        flat_grad = source_grads[level_id].reshape(seqs_dev, -1, pair_width)
        grad_left.append(flat_grad[:, :blk_rows])
        grad_own.append(flat_grad[:, blk_rows:-blk_rows])
        grad_right.append(flat_grad[:, -blk_rows:])
    group_left_grads = [
        source_grads[local_top + 1 + 2 * slot_id].reshape(seqs_dev, blk_rows, pair_width)
        for slot_id in range(levels - local_top)
    ]
    group_right_grads = [
        source_grads[local_top + 2 + 2 * slot_id].reshape(seqs_dev, blk_rows, pair_width)
        for slot_id in range(levels - local_top)
    ]
    weight_grads = [None] * levels
    carry_block = jnp.zeros((seqs_dev, blk_rows, pair_width), jnp.float32)
    carry_left = jnp.zeros((seqs_dev, 2, pair_width), jnp.float32)
    for level_id in range(levels, local_top, -1):
        slot_id = level_id - local_top - 1
        stride_dev = 2 ** (level_id - local_top)
        left_total = group_left_grads[slot_id].at[:, -2:].add(carry_left)
        block_total = (
            carry_block
            + move_grads(left_total, -stride_dev)
            + move_grads(group_right_grads[slot_id], stride_dev)
        )
        first_part = block_total[:, : blk_rows // 2]
        second_part = block_total[:, blk_rows // 2 :]
        keep_part = jnp.where(group_first[slot_id], first_part, second_part)
        give_part = jnp.where(group_first[slot_id], second_part, first_part)
        half_grad = keep_part + partner_2(give_part.astype(jnp.bfloat16), "seq", slot_id).astype(
            give_part.dtype
        )
        spread, weight_grads[level_id - 1] = coarsen_back(
            half_grad, group_extended[slot_id], kv_weight[level_id - 1]
        )
        carry_left = spread[:, :2]
        carry_block = spread[:, 2:]
    grad_left[local_top] = grad_left[local_top].at[:, -2:].add(carry_left)
    grad_own[local_top] = grad_own[local_top] + carry_block
    fine_left_conv = jnp.zeros((seqs_dev, blk_rows, pair_width), jnp.float32)
    level_id = 1
    from_right = move_grads(grad_left[level_id], -1)
    from_left = move_grads(grad_right[level_id], 1)
    level_grad = (
        grad_own[level_id].at[:, :blk_rows].add(from_left).at[:, -blk_rows:].add(from_right)
    )
    spread, weight_grads[level_id - 1] = coarsen_back(
        level_grad, extended_local[level_id], kv_weight[level_id - 1]
    )
    fine_left_conv = fine_left_conv.at[:, -2:].add(spread[:, :2])
    grad_own[level_id - 1] = grad_own[level_id - 1] + spread[:, 2:]

    def owner_terms(sent_rows, sent_stats, pair_rows):
        q_rows = sent_rows[:, :, :feat_width].reshape(seqs_dev, blk_rows, head_count, head_size)
        do_rows = sent_rows[:, :, feat_width:].reshape(seqs_dev, blk_rows, head_count, head_size)
        pair_view = pair_rows.reshape(seqs_dev, blk_rows, head_count, 2, head_size)
        raw_scores = (
            jnp.einsum(
                "bqhe,bkhe->bhqk", q_rows, pair_view[..., 0, :], preferred_element_type=jnp.float32
            )
            * score_scale
        )
        prob_full = jnp.exp(raw_scores - sent_stats[:, 0][..., None])
        grad_prob = jnp.einsum(
            "bqhe,bkhe->bhqk", do_rows, pair_view[..., 1, :], preferred_element_type=jnp.float32
        )
        dscore = (prob_full * (grad_prob - sent_stats[:, 1][..., None]) * score_scale).astype(
            jnp.bfloat16
        )
        key_grad = jnp.einsum("bhqk,bqhe->bkhe", dscore, q_rows, preferred_element_type=jnp.float32)
        value_grad = jnp.einsum(
            "bhqk,bqhe->bkhe",
            prob_full.astype(jnp.bfloat16),
            do_rows,
            preferred_element_type=jnp.float32,
        )
        return jnp.stack([key_grad, value_grad], 3).reshape(seqs_dev, blk_rows, pair_width)

    from_right = move_grads(fine_left_conv, -1)
    query_tail = jnp.concatenate([queries[:, -blk_rows:], grad_out[:, -blk_rows:]], 2)
    query_front = jnp.concatenate([queries[:, :blk_rows], grad_out[:, :blk_rows]], 2)
    stats_tail = jnp.stack([log_totals[:, -1], row_deltas[:, -1]], 1)
    stats_front = jnp.stack([log_totals[:, 0], row_deltas[:, 0]], 1)
    tail_from_left = move_near(query_tail, 1)
    front_from_right = move_near(query_front, -1)
    stats_from_left = move_grads(stats_tail, 1)
    stats_from_right = move_grads(stats_front, -1)
    left_terms = owner_terms(tail_from_left, stats_from_left, fine_pairs[:, :blk_rows])
    right_terms = owner_terms(front_from_right, stats_from_right, fine_pairs[:, -blk_rows:])
    fine_grad = (
        grad_own[0].at[:, :blk_rows].add(left_terms).at[:, -blk_rows:].add(right_terms + from_right)
    )
    grad_pairs = fine_grad.reshape(seqs_dev, tok_rows, head_count, 2, head_size)
    grad_key = (
        grad_pairs[:, :, :, 0, :].reshape(seqs_dev, tok_rows, feat_width).astype(jnp.bfloat16)
    )
    grad_value = (
        grad_pairs[:, :, :, 1, :].reshape(seqs_dev, tok_rows, feat_width).astype(jnp.bfloat16)
    )
    weight_sum = lax.psum(jnp.stack(weight_grads), ("seq", "dp")).reshape(
        levels, 4, head_count, 2, head_size
    )
    grad_conv_key = weight_sum[:, :, :, 0, :].reshape(levels, 4, feat_width)
    grad_conv_value = weight_sum[:, :, :, 1, :].reshape(levels, 4, feat_width)
    return (attended, grad_query, grad_key, grad_value, grad_conv_key, grad_conv_value)


LOG2E = 1.4426950408889634
MASKED = -1e30
EDGE = 16


def level_bases(blocks, levels):
    bases, offset = [], 0
    for level_id in range(levels + 1):
        bases.append(offset)
        offset += (blocks >> level_id) + 2
    return bases, offset


def build_levels(
    take_rows, edge, half, weight, bases, blocks, levels, wide_ref, low_ref, turned_ref
):
    zero_wide = jnp.zeros((BLOCK, HEAD_DIM), jnp.float32)
    zero_low = jnp.zeros((BLOCK, HEAD_DIM), jnp.bfloat16)
    for level_id in range(levels + 1):
        count = blocks >> level_id
        for pad in (bases[level_id], bases[level_id] + count + 1):
            wide_ref[pad * BLOCK : (pad + 1) * BLOCK] = zero_wide
        outer = bases[level_id] + half * (count + 1)
        low_ref[outer] = zero_low
        turned_ref[outer] = zero_low

    def put(index, low):
        wide = low.astype(jnp.float32)
        wide_ref[pl.ds(pl.multiple_of(index * BLOCK, BLOCK), BLOCK)] = wide
        low_ref[index] = low
        turned_ref[index] = wide.T.astype(jnp.bfloat16)

    def put_pair(distance, carry):
        pair, rows = take_rows(distance)
        put(1 + 2 * pair, rows[:BLOCK])
        put(2 + 2 * pair, rows[BLOCK:])
        return carry

    lax.fori_loop(0, blocks // 2, put_pair, 0)
    wide_ref[BLOCK - EDGE : BLOCK] = edge.astype(jnp.float32)
    for level_id in range(1, levels):
        start = (bases[level_id - 1] + 1) * BLOCK - EDGE - 2
        summed = jnp.zeros((EDGE // 2, HEAD_DIM), jnp.float32)
        for tap in range(4):
            row = 4 * (level_id - 1) + tap
            summed = summed + weight(row) * wide_ref[pl.ds(start + tap, EDGE // 2, stride=2)]
        stop = (bases[level_id] + 1) * BLOCK
        wide_ref[stop - EDGE // 2 : stop] = summed.astype(jnp.bfloat16).astype(jnp.float32)
    for level_id in range(1, levels + 1):
        for block in range(blocks >> level_id):
            start = (bases[level_id - 1] + 1 + 2 * block) * BLOCK - 2
            summed = jnp.zeros((BLOCK, HEAD_DIM), jnp.float32)
            for tap in range(4):
                row = 4 * (level_id - 1) + tap
                summed = summed + weight(row) * wide_ref[pl.ds(start + tap, BLOCK, stride=2)]
            put(bases[level_id] + 1 + block, summed.astype(jnp.bfloat16))


def attend_pair(pair, whole_pair, all_pairs, q_rows, do_rows, bases, blocks, levels, keys, values, scratch):
    key_low, key_turned, key_grad = keys
    value_low, value_turned, value_grad = values
    score_ref, dprob_ref = scratch
    scale = HEAD_DIM**-0.5
    two = 2 * BLOCK
    q_turned = q_rows.astype(jnp.float32).T.astype(jnp.bfloat16)
    do_turned = do_rows.astype(jnp.float32).T.astype(jnp.bfloat16)
    lane = lax.broadcasted_iota(jnp.int32, (1, two), 1)
    places = [2 * pair, 2 * pair + 1, 2 * pair + 2, 2 * pair + 3]
    spans = [
        (0, jnp.where(whole_pair > 0, BLOCK, 0)),
        None,
        None,
        (jnp.where(whole_pair + 1 < all_pairs, BLOCK, two), two),
    ]
    for level_id in range(1, levels + 1):
        coarse_id = pair // 2 ** (level_id - 1)
        whole_id = whole_pair // 2 ** (level_id - 1)
        places += [bases[level_id] + coarse_id, bases[level_id] + coarse_id + 2]
        spans += [
            (0, jnp.where(whole_id >= 1, two, 0)),
            (0, jnp.where(whole_id + 1 < 2 * all_pairs >> level_id, two, 0)),
        ]
    row_max = jnp.full((1, two), MASKED, jnp.float32)
    for piece, place in enumerate(places):
        score = jnp.dot(key_low[place], q_turned, preferred_element_type=jnp.float32)
        if spans[piece] is not None:
            first, last = spans[piece]
            score = jnp.where((lane >= first) & (lane < last), score, MASKED)
        score_ref[piece] = score
        row_max = jnp.maximum(row_max, jnp.max(score, 0, keepdims=True))
    total = jnp.zeros((1, two), jnp.float32)
    weighted = jnp.zeros((1, two), jnp.float32)
    for piece, place in enumerate(places):
        raised = jnp.exp2((score_ref[piece] - row_max) * (scale * LOG2E))
        dprob = jnp.dot(value_low[place], do_turned, preferred_element_type=jnp.float32)
        score_ref[piece] = raised
        dprob_ref[piece] = dprob
        total = total + jnp.sum(raised, 0, keepdims=True)
        weighted = weighted + jnp.sum(raised * dprob, 0, keepdims=True)
    inverse = 1.0 / total
    delta = weighted * inverse
    attended = jnp.zeros((HEAD_DIM, two), jnp.float32)
    grad_q = jnp.zeros((HEAD_DIM, two), jnp.float32)
    for piece in range(0, len(places), 2):
        lows, dlows = [], []
        for step in (piece, piece + 1):
            rows = pl.ds(pl.multiple_of(places[step] * BLOCK, BLOCK), BLOCK)
            probs = score_ref[step] * inverse
            probs_low = probs.astype(jnp.bfloat16)
            dscore = (probs * (dprob_ref[step] - delta)).astype(jnp.bfloat16)
            value_grad[rows] += jnp.dot(probs_low, do_rows, preferred_element_type=jnp.float32)
            key_grad[rows] += jnp.dot(dscore, q_rows, preferred_element_type=jnp.float32)
            lows.append(probs_low)
            dlows.append(dscore)
        here, there = places[piece], places[piece + 1]
        value_two = jnp.concatenate([value_turned[here], value_turned[there]], 1)
        key_two = jnp.concatenate([key_turned[here], key_turned[there]], 1)
        attended = attended + jnp.dot(
            value_two, jnp.concatenate(lows, 0), preferred_element_type=jnp.float32
        )
        grad_q = grad_q + jnp.dot(
            key_two, jnp.concatenate(dlows, 0), preferred_element_type=jnp.float32
        )
    return attended.T.astype(jnp.bfloat16), (grad_q * scale).T.astype(jnp.bfloat16)


def coarsen_gradients(weight, bases, blocks, levels, wide_ref, grad_ref, put_weight_grad):
    for level_id in range(levels, 0, -1):
        tap_sums = [jnp.zeros((1, HEAD_DIM), jnp.float32) for _ in range(4)]
        for block in range(blocks >> level_id):
            start = (bases[level_id] + 1 + block) * BLOCK
            upstream = grad_ref[start : start + BLOCK]
            following = grad_ref[start + 1 : start + 1 + BLOCK]
            below = (bases[level_id - 1] + 1 + 2 * block) * BLOCK
            taps = [weight(4 * (level_id - 1) + tap) for tap in range(4)]
            grad_ref[pl.ds(below, BLOCK, stride=2)] += taps[2] * upstream + taps[0] * following
            grad_ref[pl.ds(below + 1, BLOCK, stride=2)] += taps[3] * upstream + taps[1] * following
            for tap in range(4):
                tap_sums[tap] = tap_sums[tap] + jnp.sum(
                    upstream * wide_ref[pl.ds(below - 2 + tap, BLOCK, stride=2)], 0, keepdims=True
                )
        for tap in range(4):
            put_weight_grad(4 * (level_id - 1) + tap, tap_sums[tap])


def columns(head):
    return pl.ds(pl.multiple_of(head * HEAD_DIM, HEAD_DIM), HEAD_DIM)


def head_kernel(
    levels,
    ring,
    groups,
    q_hbm,
    key_hbm,
    value_hbm,
    do_hbm,
    conv_key_ref,
    conv_value_ref,
    att_hbm,
    grad_q_hbm,
    grad_key_hbm,
    grad_value_hbm,
    conv_key_grad,
    conv_value_grad,
    rows_ref,
    out_ref,
    conv_here,
    conv_parts,
    conv_slots,
    edge_ref,
    halo_out,
    halo_in,
    chain_out,
    chain_in,
    key_wide,
    key_low,
    key_turned,
    key_grad,
    value_wide,
    value_low,
    value_turned,
    value_grad,
    score_ref,
    dprob_ref,
    in_send,
    in_recv,
    out_send,
    out_recv,
    edge_send,
    edge_recv,
    block_send,
    block_recv,
    halo_send,
    halo_recv,
    chain_send,
    chain_recv,
    part_send,
    part_recv,
    total_send,
    total_recv,
):
    me = lax.axis_index("seq")
    group = lax.axis_index("dp")
    size = ring // 2
    heads = HEADS // size
    half = me // size
    rank = lax.rem(me, size)
    partner = lax.rem(me + size, ring)
    blocks = 2 * size
    bases, _ = level_bases(blocks, levels)
    scale = HEAD_DIM**-0.5
    sources = (q_hbm, key_hbm, value_hbm, do_hbm)
    conv_grads = (conv_key_grad, conv_value_grad)
    results = (att_hbm, grad_q_hbm, grad_key_hbm, grad_value_hbm)
    lows = (key_low, value_low)
    turned = (key_turned, value_turned)
    grads = (key_grad, value_grad)
    wides = (key_wide, value_wide)

    def after(distance):
        return lax.rem(rank + distance, size)

    def before(distance):
        return lax.rem(rank + size - distance, size)

    barrier = pltpu.get_barrier_semaphore()
    for distance in range(1, ring):
        pl.semaphore_signal(
            barrier,
            inc=1,
            device_id={"seq": lax.rem(me + distance, ring)},
            device_id_type=pl.DeviceIdType.MESH,
        )
    for distance in range(1, groups):
        pl.semaphore_signal(
            barrier,
            inc=1,
            device_id={"dp": lax.rem(group + distance, groups)},
            device_id_type=pl.DeviceIdType.MESH,
        )
    pl.semaphore_wait(barrier, ring + groups - 2)

    def to_seq(source, target, send_sem, recv_sem, device):
        return pltpu.make_async_remote_copy(
            src_ref=source,
            dst_ref=target,
            send_sem=send_sem,
            recv_sem=recv_sem,
            device_id={"seq": device},
            device_id_type=pl.DeviceIdType.MESH,
        )

    def inbound(array, distance, head, landing):
        place = (array, distance, head)
        return to_seq(
            sources[array].at[0, :, columns(after(distance) * heads + head)],
            rows_ref.at[landing, array, head],
            in_send.at[place],
            in_recv.at[place],
            half * size + after(distance),
        )

    def inbound_own(array, head):
        return pltpu.make_async_copy(
            sources[array].at[0, :, columns(rank * heads + head)],
            rows_ref.at[rank, array, head],
            in_recv.at[array, 0, head],
        )

    def outbound(array, distance, head, origin):
        place = (array, distance, head)
        return to_seq(
            out_ref.at[before(distance), array, head],
            results[array].at[0, :, columns(origin * heads + head)],
            out_send.at[place],
            out_recv.at[place],
            half * size + before(distance),
        )

    def outbound_own(array, head):
        return pltpu.make_async_copy(
            out_ref.at[rank, array, head],
            results[array].at[0, :, columns(rank * heads + head)],
            out_recv.at[array, 0, head],
        )

    def edge_copy(kind, head, other):
        return to_seq(
            sources[1 + kind].at[0, pl.ds(2 * BLOCK - EDGE, EDGE), columns(other * heads + head)],
            edge_ref.at[kind, head],
            edge_send.at[kind, head, other],
            edge_recv.at[kind, head],
            size + other,
        )

    def edge_place(level_id):
        count = blocks >> level_id
        return bases[level_id] + count - half * (count - 1)

    def pad_place(level_id, of_half):
        return bases[level_id] + (1 - of_half) * ((blocks >> level_id) + 1)

    def block_copy(kind, level_id, head, pad):
        place = (kind, level_id, head)
        return to_seq(
            lows[kind].at[head, edge_place(level_id)],
            lows[kind].at[head, pad],
            block_send.at[place],
            block_recv.at[place],
            partner,
        )

    def halo_copy(kind, level_id, head):
        place = (kind, level_id, head)
        return to_seq(
            halo_out.at[place], halo_in.at[place], halo_send.at[place], halo_recv.at[place], partner
        )

    def chain_copy(kind, head):
        return to_seq(
            chain_out.at[kind, head],
            chain_in.at[kind, head],
            chain_send.at[kind, head],
            chain_recv.at[kind, head],
            partner,
        )

    every = [(kind, head) for kind in range(2) for head in range(heads)]

    @pl.when(me == size - 1)
    def _():
        for kind, head in every:
            for other in range(size):
                edge_copy(kind, head, other).start()

    @pl.when(half == 0)
    def _():
        edge_ref[...] = jnp.zeros_like(edge_ref)

    def send(*arrays):
        for array in arrays:
            for head in range(heads):
                inbound_own(array, head).start()

        def step(distance, carry):
            for array in arrays:
                for head in range(heads):
                    inbound(array, distance, head, rank).start()
            return carry

        lax.fori_loop(1, size, step, 0)

    send(1)
    send(2)
    for head in range(heads):
        conv_here[0, head] = conv_key_ref[:, :, columns(rank * heads + head)]
        conv_here[1, head] = conv_value_ref[:, :, columns(rank * heads + head)]

    def arrived(array, distance, head):
        @pl.when(distance == 0)
        def _():
            inbound_own(array, head).wait()

        @pl.when(distance > 0)
        def _():
            inbound(array, distance, head, before(distance)).wait_recv()

    def leave(array, distance, head):
        @pl.when(distance == 0)
        def _():
            outbound_own(array, head).start()

        @pl.when(distance > 0)
        def _():
            outbound(array, distance, head, rank).start()

    def taker(array, head):
        def take_rows(distance):
            arrived(array, distance, head)
            return before(distance), rows_ref[before(distance), array, head]

        return take_rows

    def weight_of(kind, head):
        def weight(row):
            return conv_here[kind, head, row // 4, row % 4 : row % 4 + 1]

        return weight

    shape = (bases, blocks, levels)
    key_grad[...] = jnp.zeros_like(key_grad)
    value_grad[...] = jnp.zeros_like(value_grad)

    @pl.when(half == 1)
    def _():
        for kind, head in every:
            edge_copy(kind, head, rank).wait_recv()

    for kind in range(2):
        for head in range(heads):
            build_levels(
                taker(1 + kind, head),
                edge_ref[kind, head],
                half,
                weight_of(kind, head),
                *shape,
                wides[kind].at[head],
                lows[kind].at[head],
                turned[kind].at[head],
            )
            for level_id in range(levels, -1, -1):
                block_copy(kind, level_id, head, pad_place(level_id, 1 - half)).start()
        if kind == 0:
            send(0, 3)
    for kind, head in every:
        for level_id in range(levels, -1, -1):
            pad = pad_place(level_id, half)
            block_copy(kind, level_id, head, pad).wait_recv()
            wide = lows[kind][head, pad].astype(jnp.float32)
            turned[kind][head, pad] = wide.T.astype(jnp.bfloat16)

    def step(index, carry):
        count = index // heads
        head = lax.rem(index, heads)
        pair = (1 - half) * (size - 1 - count) + half * count
        distance = lax.rem(rank + size - pair, size)
        arrived(0, distance, head)
        arrived(3, distance, head)
        attended, grad_q = attend_pair(
            pair,
            half * size + pair,
            ring,
            rows_ref[pair, 0, head],
            rows_ref[pair, 3, head],
            *shape,
            (key_low.at[head], key_turned.at[head], key_grad.at[head]),
            (value_low.at[head], value_turned.at[head], value_grad.at[head]),
            (score_ref, dprob_ref),
        )
        out_ref[pair, 0, head] = attended
        out_ref[pair, 1, head] = grad_q
        leave(0, distance, head)
        leave(1, distance, head)
        for level_id in range(levels + 1):

            @pl.when(count == max(1, 1 << level_id >> 1) - 1)
            def _(level_id=level_id):
                start = pl.multiple_of(pad_place(level_id, half) * BLOCK, BLOCK)
                for kind in range(2):
                    rows = grads[kind][head, pl.ds(start, BLOCK)]
                    halo_out[kind, level_id, head] = rows.astype(jnp.bfloat16)
                    halo_copy(kind, level_id, head).start()

        return carry

    lax.fori_loop(0, size * heads, step, 0)

    for kind, head in every:
        for level_id in range(levels + 1):
            halo_copy(kind, level_id, head).wait_recv()
            rows = pl.ds(pl.multiple_of(edge_place(level_id) * BLOCK, BLOCK), BLOCK)
            grads[kind][head, rows] += halo_in[kind, level_id, head].astype(jnp.float32)

    def finisher(array, head, grad_ref, factor):
        def finish(distance, carry):
            pair = before(distance)
            rows = pl.ds(pl.multiple_of((1 + 2 * pair) * BLOCK, BLOCK), 2 * BLOCK)
            out_ref[pair, array, head] = (grad_ref[head, rows] * factor).astype(jnp.bfloat16)
            leave(array, distance, head)
            return carry

        return finish

    for kind, head in every:
        grad_ref = grads[kind].at[head]

        @pl.when(half == 0)
        def _(kind=kind, head=head, grad_ref=grad_ref):
            chain_copy(kind, head).wait_recv()
            for level_id in range(1, levels + 1):
                start = (bases[level_id] + (blocks >> level_id) + 1) * BLOCK
                grad_ref[start : start + 8] = chain_in[kind, head, level_id - 1]

        def put(row, value, kind=kind, head=head):
            factor = 1.0 if kind else scale
            here = slice(head * HEAD_DIM, (head + 1) * HEAD_DIM)
            conv_parts[group, kind, row // 4, row % 4 : row % 4 + 1, here] = value * factor

        coarsen_gradients(weight_of(kind, head), *shape, wides[kind].at[head], grad_ref, put)

        @pl.when(half == 1)
        def _(kind=kind, head=head, grad_ref=grad_ref):
            for level_id in range(1, levels + 1):
                start = (bases[level_id] + 1) * BLOCK
                chain_out[kind, head, level_id - 1] = grad_ref[start : start + 8]
            chain_copy(kind, head).start()

        lax.fori_loop(0, size, finisher(2 + kind, head, grads[kind], 1.0 if kind else scale), 0)

    def part(distance, slot):
        return pltpu.make_async_remote_copy(
            src_ref=conv_parts.at[group],
            dst_ref=conv_parts.at[slot],
            send_sem=part_send.at[distance],
            recv_sem=part_recv.at[distance],
            device_id={"dp": lax.rem(group + distance, groups)},
            device_id_type=pl.DeviceIdType.MESH,
        )

    def gathered(distance, slot):
        return to_seq(
            conv_slots.at[me],
            conv_slots.at[slot],
            total_send.at[distance],
            total_recv.at[distance],
            lax.rem(me + distance, ring),
        )

    for distance in range(1, groups):
        part(distance, group).start()
    for distance in range(1, groups):
        part(distance, lax.rem(group + groups - distance, groups)).wait_recv()
    conv_sum = conv_parts[0]
    for slot in range(1, groups):
        conv_sum = conv_sum + conv_parts[slot]
    conv_slots[me] = conv_sum
    for distance in range(1, ring):
        gathered(distance, me).start()
    for distance in range(1, ring):
        gathered(distance, lax.rem(me + ring - distance, ring)).wait_recv()
    width = heads * HEAD_DIM
    for kind in range(2):
        for slot in range(size):
            both = conv_slots[slot, kind] + conv_slots[size + slot, kind]
            conv_grads[kind][:, :, slot * width : (slot + 1) * width] = both

    for array in range(4):
        for head in range(heads):
            outbound_own(array, head).wait()

    def settle(distance, carry):
        for array in range(4):
            for head in range(heads):
                inbound(array, distance, head, rank).wait_send()
                outbound(array, distance, head, rank).wait_send()
                outbound(array, distance, head, after(distance)).wait_recv()
        return carry

    lax.fori_loop(1, size, settle, 0)
    for distance in range(1, ring):
        gathered(distance, me).wait_send()
    for distance in range(1, groups):
        part(distance, group).wait_send()
    for kind, head in every:
        for level_id in range(levels + 1):
            block_copy(kind, level_id, head, pad_place(level_id, 1 - half)).wait_send()
            halo_copy(kind, level_id, head).wait_send()

    @pl.when(half == 1)
    def _():
        for kind, head in every:
            chain_copy(kind, head).wait_send()

    @pl.when(me == size - 1)
    def _():
        for kind, head in every:
            for other in range(size):
                edge_copy(kind, head, other).wait_send()


def stack_scratch(heads, blocks, levels):
    total = level_bases(blocks, levels)[1]
    flat = pltpu.VMEM((heads, total * BLOCK, HEAD_DIM), jnp.float32)
    low = pltpu.VMEM((heads, total, BLOCK, HEAD_DIM), jnp.bfloat16)
    return [flat, low, low, flat]


def per_device_heads(queries, key_rows, value_rows, conv_key, conv_value, grad_out):
    tok_rows = queries.shape[1]
    levels = conv_key.shape[0]
    ring, groups = lax.axis_size("seq"), lax.axis_size("dp")
    size = ring // 2
    heads = HEADS // size
    like = jax.ShapeDtypeStruct(queries.shape, jnp.bfloat16)
    conv_like = jax.ShapeDtypeStruct(conv_key.shape, jnp.float32)
    scores = pltpu.VMEM((4 + 2 * levels, BLOCK, 2 * BLOCK), jnp.float32)
    rows = pltpu.VMEM((size, 4, heads, tok_rows, HEAD_DIM), jnp.bfloat16)
    conv_part = (2, levels, 4, heads * HEAD_DIM)
    halo = pltpu.VMEM((2, levels + 1, heads, BLOCK, HEAD_DIM), jnp.bfloat16)
    chain = pltpu.VMEM((2, heads, levels, 8, HEAD_DIM), jnp.float32)
    dma = pltpu.SemaphoreType.DMA
    in_hbm = pl.BlockSpec(memory_space=pltpu.HBM)
    anywhere = pl.BlockSpec(memory_space=pl.ANY)
    in_vmem = pl.BlockSpec(memory_space=pltpu.VMEM)
    return pl.pallas_call(
        functools.partial(head_kernel, levels, ring, groups),
        out_shape=(like, like, like, like, conv_like, conv_like),
        in_specs=[in_hbm] * 4 + [in_vmem] * 2,
        out_specs=[anywhere] * 4 + [in_vmem] * 2,
        scratch_shapes=[
            rows,
            rows,
            pltpu.VMEM((2, heads, levels, 4, HEAD_DIM), jnp.float32),
            pltpu.VMEM((groups,) + conv_part, jnp.float32),
            pltpu.VMEM((ring,) + conv_part, jnp.float32),
            pltpu.VMEM((2, heads, EDGE, HEAD_DIM), jnp.bfloat16),
            halo,
            halo,
            chain,
            chain,
        ]
        + stack_scratch(heads, 2 * size, levels) * 2
        + [scores, scores]
        + [dma((4, size, heads))] * 4
        + [dma((2, heads, size)), dma((2, heads))]
        + [dma((2, levels + 1, heads))] * 4
        + [dma((2, heads))] * 2
        + [dma((groups,))] * 2
        + [dma((ring,))] * 2,
        compiler_params=pltpu.CompilerParams(
            collective_id=0, has_side_effects=True, vmem_limit_bytes=48 * 2**20
        ),
    )(queries, key_rows, value_rows, grad_out, conv_key, conv_value)


def solution(mesh):
    in_specs = (
        P("dp", "seq", None),
        P("dp", "seq", None),
        P("dp", "seq", None),
        P(),
        P(),
        P("dp", "seq", None),
    )
    out_specs = (
        P("dp", "seq", None),
        P("dp", "seq", None),
        P("dp", "seq", None),
        P("dp", "seq", None),
        P(),
        P(),
    )
    def chosen(*args):
        seq_devices = lax.axis_size("seq")
        fits = seq_devices == HEADS and args[0].shape[:2] == (1, 2 * BLOCK)
        fits = fits and seq_devices >> args[3].shape[0] >= 1
        return (per_device_heads if fits else per_device)(*args)

    return jax.shard_map(
        chosen, mesh=mesh, in_specs=in_specs, out_specs=out_specs, check_vma=False
    )
```

```python
import functools

import jax
import jax.numpy as jnp
from jax import lax
from jax.experimental import pallas as pl
from jax.experimental.pallas import tpu as pltpu
from jax.sharding import PartitionSpec as P

HEADS = 8
HEAD_DIM = 128
BLOCK = 128


def passed_along(value, axis, steps):
    count = lax.axis_size(axis)
    initial, last = (max(0, -steps), min(count, count - steps))
    return lax.ppermute(value, axis, [(source, source + steps) for source in range(initial, last)])


def partner_2(array, axis, distance):
    return lax.ppermute(array, axis, [(i, i ^ 1 << distance) for i in range(lax.axis_size(axis))])


def coarsen(extended, weight):
    out_rows = (extended.shape[1] - 2) // 2
    summed = weight[0] * extended[:, 0 : 2 * out_rows : 2].astype(jnp.float32)
    for offset in range(1, 4):
        summed = summed + weight[offset] * extended[:, offset : offset + 2 * out_rows : 2].astype(
            jnp.float32
        )
    return summed.astype(jnp.bfloat16)


def coarsen_back(upstream, extended, weight):
    seqs_dev, out_rows, feat_width = upstream.shape
    zero_row = jnp.zeros((seqs_dev, 1, feat_width), jnp.float32)
    even_rows = jnp.concatenate([weight[0] * upstream, zero_row], 1) + jnp.concatenate(
        [zero_row, weight[2] * upstream], 1
    )
    odd_rows = jnp.concatenate([weight[1] * upstream, zero_row], 1) + jnp.concatenate(
        [zero_row, weight[3] * upstream], 1
    )
    spread = jnp.stack([even_rows, odd_rows], 2).reshape(seqs_dev, 2 * out_rows + 2, feat_width)
    weight_grad = jnp.stack(
        [
            jnp.sum(
                upstream * extended[:, offset : offset + 2 * out_rows : 2].astype(jnp.float32),
                (0, 1),
            )
            for offset in range(4)
        ]
    )
    return (spread, weight_grad)


def move_near(moved_rows, shift_by):
    return passed_along(moved_rows, "seq", shift_by)


def move_grads(moved_rows, shift_by):
    return passed_along(moved_rows.astype(jnp.bfloat16), "seq", shift_by).astype(moved_rows.dtype)


def per_device(queries, key_rows, value_rows, conv_key, conv_value, grad_out):
    seqs_dev, tok_rows, feat_width = queries.shape
    levels = conv_key.shape[0]
    head_count = HEADS
    head_size = HEAD_DIM
    blk_rows = BLOCK
    blocks_here = tok_rows // blk_rows
    local_top = blocks_here.bit_length() - 1
    seq_devices = lax.axis_size("seq")
    dev_index = lax.axis_index("seq")
    total_blocks = blocks_here * seq_devices
    score_scale = head_size ** (-0.5)
    pair_width = 2 * feat_width
    group_heads = 2
    kv_weight = jnp.stack(
        [
            conv_key.reshape(levels, 4, head_count, head_size),
            conv_value.reshape(levels, 4, head_count, head_size),
        ],
        3,
    ).reshape(levels, 4, pair_width)
    fine_pairs = jnp.stack(
        [
            key_rows.reshape(seqs_dev, tok_rows, head_count, head_size),
            value_rows.reshape(seqs_dev, tok_rows, head_count, head_size),
        ],
        3,
    ).reshape(seqs_dev, tok_rows, pair_width)
    own_rows = [fine_pairs]
    left_rims = [move_near(fine_pairs[:, -blk_rows:], 1)]
    right_rims = [move_near(fine_pairs[:, :blk_rows], -1)]
    extended_local = [None]
    level_id = 1
    extended = jnp.concatenate([left_rims[level_id - 1][:, -2:], own_rows[level_id - 1]], 1)
    extended_local.append(extended)
    coarse = coarsen(extended, kv_weight[level_id - 1])
    own_rows.append(coarse)
    left_rims.append(move_near(coarse, 1))
    right_rims.append(move_near(coarse, -1))
    block_now = own_rows[local_top]
    left_now = left_rims[local_top]
    group_lefts, group_rights, group_extended, group_first = ([], [], [], [])
    for level_id in range(local_top + 1, levels + 1):
        swap_bit = level_id - local_top - 1
        extended = jnp.concatenate([left_now[:, -2:], block_now], 1)
        group_extended.append(extended)
        own_half = coarsen(extended, kv_weight[level_id - 1])
        partner = partner_2(own_half, "seq", swap_bit)
        is_first = dev_index // 2**swap_bit % 2 == 0
        group_first.append(is_first)
        block_now = jnp.where(
            is_first,
            jnp.concatenate([own_half, partner], 1),
            jnp.concatenate([partner, own_half], 1),
        )
        stride_dev = 2 ** (level_id - local_top)
        left_now = move_near(block_now, stride_dev)
        right_now = move_near(block_now, -stride_dev)
        group_lefts.append(left_now)
        group_rights.append(right_now)
    glob_blocks = dev_index * blocks_here + jnp.arange(blocks_here, dtype=jnp.int32)
    always = jnp.ones((blocks_here,), jnp.bool_)
    sources = []
    pieces = []
    for level_id in range(local_top + 1):
        block_count = blocks_here >> level_id
        padded = jnp.concatenate([left_rims[level_id], own_rows[level_id], right_rims[level_id]], 1)
        sources.append(
            padded.reshape(seqs_dev, block_count + 2, blk_rows, head_count, 2, head_size)
        )
        coarse_id = glob_blocks // 2**level_id
        spread = 2**level_id
        pieces.append((level_id, 0, spread, coarse_id >= 1))
        if level_id == 0:
            pieces.append((0, 1, 1, always))
        pieces.append((level_id, 2, spread, coarse_id + 1 < total_blocks // 2**level_id))
    for slot_id in range(levels - local_top):
        level_id = local_top + 1 + slot_id
        coarse_id = glob_blocks // 2**level_id
        sources.append(
            group_lefts[slot_id].reshape(seqs_dev, 1, blk_rows, head_count, 2, head_size)
        )
        pieces.append((len(sources) - 1, 0, blocks_here, coarse_id >= 1))
        sources.append(
            group_rights[slot_id].reshape(seqs_dev, 1, blk_rows, head_count, 2, head_size)
        )
        pieces.append(
            (len(sources) - 1, 0, blocks_here, coarse_id + 1 < total_blocks // 2**level_id)
        )
    query_blocks = queries.reshape(seqs_dev, blocks_here, blk_rows, head_count, head_size)
    out_blocks = grad_out.reshape(seqs_dev, blocks_here, blk_rows, head_count, head_size)

    def head_group(group_id, loop_state):
        attended_acc, grad_q_acc, source_grads, log_totals, row_deltas = loop_state
        head_start = group_id * group_heads
        q_part = lax.dynamic_slice_in_dim(query_blocks, head_start, group_heads, 3)
        do_part = lax.dynamic_slice_in_dim(out_blocks, head_start, group_heads, 3)
        source_parts = [
            lax.dynamic_slice_in_dim(source, head_start, group_heads, 3) for source in sources
        ]
        score_list = []
        views = []
        for source_id, offset, spread, valid_mask in pieces:
            block_count = blocks_here // spread
            key_blocks = source_parts[source_id][:, offset : offset + block_count]
            q_view = q_part.reshape(seqs_dev, block_count, spread, blk_rows, group_heads, head_size)
            do_view = do_part.reshape(
                seqs_dev, block_count, spread, blk_rows, group_heads, head_size
            )
            raw_scores = jnp.einsum(
                "bnrqhe,bnkhe->bnrhqk",
                q_view,
                key_blocks[..., 0, :],
                preferred_element_type=jnp.float32,
            )
            raw_scores = (
                raw_scores.reshape(seqs_dev, blocks_here, group_heads, blk_rows, blk_rows)
                * score_scale
            )
            score_list.append(
                jnp.where(valid_mask[None, :, None, None, None], raw_scores, -jnp.inf)
            )
            views.append((key_blocks, q_view, do_view, block_count, spread))
        all_scores = jnp.concatenate(score_list, 4)
        row_max = jnp.max(all_scores, 4, keepdims=True)
        exp_scores = jnp.exp(all_scores - row_max)
        summed = jnp.sum(exp_scores, 4, keepdims=True)
        prob_full = exp_scores / summed
        probs_low = prob_full.astype(jnp.bfloat16)
        attended_part = jnp.zeros(
            (seqs_dev, blocks_here, blk_rows, group_heads, head_size), jnp.float32
        )
        grad_prob_list = []
        for piece_id, (key_blocks, q_view, do_view, block_count, spread) in enumerate(views):
            p_slice = probs_low[..., piece_id * blk_rows : (piece_id + 1) * blk_rows].reshape(
                seqs_dev, block_count, spread, group_heads, blk_rows, blk_rows
            )
            attended_part = attended_part + jnp.einsum(
                "bnrhqk,bnkhe->bnrqhe",
                p_slice,
                key_blocks[..., 1, :],
                preferred_element_type=jnp.float32,
            ).reshape(attended_part.shape)
            grad_prob = jnp.einsum(
                "bnrqhe,bnkhe->bnrhqk",
                do_view,
                key_blocks[..., 1, :],
                preferred_element_type=jnp.float32,
            )
            grad_prob_list.append(
                grad_prob.reshape(seqs_dev, blocks_here, group_heads, blk_rows, blk_rows)
            )
        grad_prob_all = jnp.concatenate(grad_prob_list, 4)
        row_delta = jnp.sum(prob_full * grad_prob_all, 4, keepdims=True)
        dscore = (prob_full * (grad_prob_all - row_delta) * score_scale).astype(jnp.bfloat16)
        grad_q_part = jnp.zeros(
            (seqs_dev, blocks_here, blk_rows, group_heads, head_size), jnp.float32
        )
        group_grads = [jnp.zeros(part_arr.shape, jnp.float32) for part_arr in source_parts]
        for piece_id, (key_blocks, q_view, do_view, block_count, spread) in enumerate(views):
            source_id, offset = (pieces[piece_id][0], pieces[piece_id][1])
            p_slice = probs_low[..., piece_id * blk_rows : (piece_id + 1) * blk_rows].reshape(
                seqs_dev, block_count, spread, group_heads, blk_rows, blk_rows
            )
            ds_slice = dscore[..., piece_id * blk_rows : (piece_id + 1) * blk_rows].reshape(
                seqs_dev, block_count, spread, group_heads, blk_rows, blk_rows
            )
            grad_q_part = grad_q_part + jnp.einsum(
                "bnrhqk,bnkhe->bnrqhe",
                ds_slice,
                key_blocks[..., 0, :],
                preferred_element_type=jnp.float32,
            ).reshape(grad_q_part.shape)
            key_grad = jnp.einsum(
                "bnrhqk,bnrqhe->bnkhe", ds_slice, q_view, preferred_element_type=jnp.float32
            )
            value_grad = jnp.einsum(
                "bnrhqk,bnrqhe->bnkhe", p_slice, do_view, preferred_element_type=jnp.float32
            )
            pair_grad = jnp.stack([key_grad, value_grad], 4)
            group_grads[source_id] = (
                group_grads[source_id].at[:, offset : offset + block_count].add(pair_grad)
            )
        attended_acc = lax.dynamic_update_slice_in_dim(
            attended_acc, attended_part.astype(jnp.bfloat16), head_start, 3
        )
        grad_q_acc = lax.dynamic_update_slice_in_dim(
            grad_q_acc, grad_q_part.astype(jnp.bfloat16), head_start, 3
        )
        source_grads = tuple(
            (
                lax.dynamic_update_slice_in_dim(whole, group_part, head_start, 3)
                for whole, group_part in zip(source_grads, group_grads)
            )
        )
        log_totals = lax.dynamic_update_slice_in_dim(
            log_totals, (row_max + jnp.log(summed))[..., 0], head_start, 2
        )
        row_deltas = lax.dynamic_update_slice_in_dim(row_deltas, row_delta[..., 0], head_start, 2)
        return (attended_acc, grad_q_acc, source_grads, log_totals, row_deltas)

    start_state = (
        jnp.zeros((seqs_dev, blocks_here, blk_rows, head_count, head_size), jnp.bfloat16),
        jnp.zeros((seqs_dev, blocks_here, blk_rows, head_count, head_size), jnp.bfloat16),
        tuple((jnp.zeros(source.shape, jnp.float32) for source in sources)),
        jnp.zeros((seqs_dev, blocks_here, head_count, blk_rows), jnp.float32),
        jnp.zeros((seqs_dev, blocks_here, head_count, blk_rows), jnp.float32),
    )
    attended_acc, grad_q_acc, source_grads, log_totals, row_deltas = lax.fori_loop(
        0, head_count // group_heads, head_group, start_state
    )
    attended = attended_acc.reshape(seqs_dev, tok_rows, feat_width)
    grad_query = grad_q_acc.reshape(seqs_dev, tok_rows, feat_width)
    grad_left, grad_own, grad_right = ([], [], [])
    for level_id in range(local_top + 1):
        flat_grad = source_grads[level_id].reshape(seqs_dev, -1, pair_width)
        grad_left.append(flat_grad[:, :blk_rows])
        grad_own.append(flat_grad[:, blk_rows:-blk_rows])
        grad_right.append(flat_grad[:, -blk_rows:])
    group_left_grads = [
        source_grads[local_top + 1 + 2 * slot_id].reshape(seqs_dev, blk_rows, pair_width)
        for slot_id in range(levels - local_top)
    ]
    group_right_grads = [
        source_grads[local_top + 2 + 2 * slot_id].reshape(seqs_dev, blk_rows, pair_width)
        for slot_id in range(levels - local_top)
    ]
    weight_grads = [None] * levels
    carry_block = jnp.zeros((seqs_dev, blk_rows, pair_width), jnp.float32)
    carry_left = jnp.zeros((seqs_dev, 2, pair_width), jnp.float32)
    for level_id in range(levels, local_top, -1):
        slot_id = level_id - local_top - 1
        stride_dev = 2 ** (level_id - local_top)
        left_total = group_left_grads[slot_id].at[:, -2:].add(carry_left)
        block_total = (
            carry_block
            + move_grads(left_total, -stride_dev)
            + move_grads(group_right_grads[slot_id], stride_dev)
        )
        first_part = block_total[:, : blk_rows // 2]
        second_part = block_total[:, blk_rows // 2 :]
        keep_part = jnp.where(group_first[slot_id], first_part, second_part)
        give_part = jnp.where(group_first[slot_id], second_part, first_part)
        half_grad = keep_part + partner_2(give_part.astype(jnp.bfloat16), "seq", slot_id).astype(
            give_part.dtype
        )
        spread, weight_grads[level_id - 1] = coarsen_back(
            half_grad, group_extended[slot_id], kv_weight[level_id - 1]
        )
        carry_left = spread[:, :2]
        carry_block = spread[:, 2:]
    grad_left[local_top] = grad_left[local_top].at[:, -2:].add(carry_left)
    grad_own[local_top] = grad_own[local_top] + carry_block
    fine_left_conv = jnp.zeros((seqs_dev, blk_rows, pair_width), jnp.float32)
    level_id = 1
    from_right = move_grads(grad_left[level_id], -1)
    from_left = move_grads(grad_right[level_id], 1)
    level_grad = (
        grad_own[level_id].at[:, :blk_rows].add(from_left).at[:, -blk_rows:].add(from_right)
    )
    spread, weight_grads[level_id - 1] = coarsen_back(
        level_grad, extended_local[level_id], kv_weight[level_id - 1]
    )
    fine_left_conv = fine_left_conv.at[:, -2:].add(spread[:, :2])
    grad_own[level_id - 1] = grad_own[level_id - 1] + spread[:, 2:]

    def owner_terms(sent_rows, sent_stats, pair_rows):
        q_rows = sent_rows[:, :, :feat_width].reshape(seqs_dev, blk_rows, head_count, head_size)
        do_rows = sent_rows[:, :, feat_width:].reshape(seqs_dev, blk_rows, head_count, head_size)
        pair_view = pair_rows.reshape(seqs_dev, blk_rows, head_count, 2, head_size)
        raw_scores = (
            jnp.einsum(
                "bqhe,bkhe->bhqk", q_rows, pair_view[..., 0, :], preferred_element_type=jnp.float32
            )
            * score_scale
        )
        prob_full = jnp.exp(raw_scores - sent_stats[:, 0][..., None])
        grad_prob = jnp.einsum(
            "bqhe,bkhe->bhqk", do_rows, pair_view[..., 1, :], preferred_element_type=jnp.float32
        )
        dscore = (prob_full * (grad_prob - sent_stats[:, 1][..., None]) * score_scale).astype(
            jnp.bfloat16
        )
        key_grad = jnp.einsum("bhqk,bqhe->bkhe", dscore, q_rows, preferred_element_type=jnp.float32)
        value_grad = jnp.einsum(
            "bhqk,bqhe->bkhe",
            prob_full.astype(jnp.bfloat16),
            do_rows,
            preferred_element_type=jnp.float32,
        )
        return jnp.stack([key_grad, value_grad], 3).reshape(seqs_dev, blk_rows, pair_width)

    from_right = move_grads(fine_left_conv, -1)
    query_tail = jnp.concatenate([queries[:, -blk_rows:], grad_out[:, -blk_rows:]], 2)
    query_front = jnp.concatenate([queries[:, :blk_rows], grad_out[:, :blk_rows]], 2)
    stats_tail = jnp.stack([log_totals[:, -1], row_deltas[:, -1]], 1)
    stats_front = jnp.stack([log_totals[:, 0], row_deltas[:, 0]], 1)
    tail_from_left = move_near(query_tail, 1)
    front_from_right = move_near(query_front, -1)
    stats_from_left = move_grads(stats_tail, 1)
    stats_from_right = move_grads(stats_front, -1)
    left_terms = owner_terms(tail_from_left, stats_from_left, fine_pairs[:, :blk_rows])
    right_terms = owner_terms(front_from_right, stats_from_right, fine_pairs[:, -blk_rows:])
    fine_grad = (
        grad_own[0].at[:, :blk_rows].add(left_terms).at[:, -blk_rows:].add(right_terms + from_right)
    )
    grad_pairs = fine_grad.reshape(seqs_dev, tok_rows, head_count, 2, head_size)
    grad_key = (
        grad_pairs[:, :, :, 0, :].reshape(seqs_dev, tok_rows, feat_width).astype(jnp.bfloat16)
    )
    grad_value = (
        grad_pairs[:, :, :, 1, :].reshape(seqs_dev, tok_rows, feat_width).astype(jnp.bfloat16)
    )
    weight_sum = lax.psum(jnp.stack(weight_grads), ("seq", "dp")).reshape(
        levels, 4, head_count, 2, head_size
    )
    grad_conv_key = weight_sum[:, :, :, 0, :].reshape(levels, 4, feat_width)
    grad_conv_value = weight_sum[:, :, :, 1, :].reshape(levels, 4, feat_width)
    return (attended, grad_query, grad_key, grad_value, grad_conv_key, grad_conv_value)


LOG2E = 1.4426950408889634
MASKED = -1e30
EDGE = 16


def level_bases(blocks, levels):
    bases, offset = [], 0
    for level_id in range(levels + 1):
        bases.append(offset)
        offset += (blocks >> level_id) + 2
    return bases, offset


def build_levels(
    take_rows, edge, half, weight, bases, blocks, levels, wide_ref, low_ref, turned_ref
):
    zero_wide = jnp.zeros((BLOCK, HEAD_DIM), jnp.float32)
    zero_low = jnp.zeros((BLOCK, HEAD_DIM), jnp.bfloat16)
    for level_id in range(levels + 1):
        count = blocks >> level_id
        for pad in (bases[level_id], bases[level_id] + count + 1):
            wide_ref[pad * BLOCK : (pad + 1) * BLOCK] = zero_wide
        outer = bases[level_id] + half * (count + 1)
        low_ref[outer] = zero_low
        turned_ref[outer] = zero_low

    def put(index, low):
        wide = low.astype(jnp.float32)
        wide_ref[pl.ds(pl.multiple_of(index * BLOCK, BLOCK), BLOCK)] = wide
        low_ref[index] = low
        turned_ref[index] = wide.T.astype(jnp.bfloat16)

    def put_pair(distance, carry):
        pair, rows = take_rows(distance)
        put(1 + 2 * pair, rows[:BLOCK])
        put(2 + 2 * pair, rows[BLOCK:])
        return carry

    lax.fori_loop(0, blocks // 2, put_pair, 0)
    wide_ref[BLOCK - EDGE : BLOCK] = edge.astype(jnp.float32)
    for level_id in range(1, levels):
        start = (bases[level_id - 1] + 1) * BLOCK - EDGE - 2
        summed = jnp.zeros((EDGE // 2, HEAD_DIM), jnp.float32)
        for tap in range(4):
            row = 4 * (level_id - 1) + tap
            summed = summed + weight(row) * wide_ref[pl.ds(start + tap, EDGE // 2, stride=2)]
        stop = (bases[level_id] + 1) * BLOCK
        wide_ref[stop - EDGE // 2 : stop] = summed.astype(jnp.bfloat16).astype(jnp.float32)
    for level_id in range(1, levels + 1):
        for block in range(blocks >> level_id):
            start = (bases[level_id - 1] + 1 + 2 * block) * BLOCK - 2
            summed = jnp.zeros((BLOCK, HEAD_DIM), jnp.float32)
            for tap in range(4):
                row = 4 * (level_id - 1) + tap
                summed = summed + weight(row) * wide_ref[pl.ds(start + tap, BLOCK, stride=2)]
            put(bases[level_id] + 1 + block, summed.astype(jnp.bfloat16))


def attend_pair(pair, whole_pair, all_pairs, q_rows, do_rows, bases, blocks, levels, keys, values, scratch):
    key_low, key_turned, key_grad = keys
    value_low, value_turned, value_grad = values
    score_ref, dprob_ref = scratch
    scale = HEAD_DIM**-0.5
    two = 2 * BLOCK
    q_turned = q_rows.astype(jnp.float32).T.astype(jnp.bfloat16)
    do_turned = do_rows.astype(jnp.float32).T.astype(jnp.bfloat16)
    lane = lax.broadcasted_iota(jnp.int32, (1, two), 1)
    places = [2 * pair, 2 * pair + 1, 2 * pair + 2, 2 * pair + 3]
    spans = [
        (0, jnp.where(whole_pair > 0, BLOCK, 0)),
        None,
        None,
        (jnp.where(whole_pair + 1 < all_pairs, BLOCK, two), two),
    ]
    for level_id in range(1, levels + 1):
        coarse_id = pair // 2 ** (level_id - 1)
        whole_id = whole_pair // 2 ** (level_id - 1)
        places += [bases[level_id] + coarse_id, bases[level_id] + coarse_id + 2]
        spans += [
            (0, jnp.where(whole_id >= 1, two, 0)),
            (0, jnp.where(whole_id + 1 < 2 * all_pairs >> level_id, two, 0)),
        ]
    row_max = jnp.full((1, two), MASKED, jnp.float32)
    for piece, place in enumerate(places):
        score = jnp.dot(key_low[place], q_turned, preferred_element_type=jnp.float32)
        if spans[piece] is not None:
            first, last = spans[piece]
            score = jnp.where((lane >= first) & (lane < last), score, MASKED)
        score_ref[piece] = score
        row_max = jnp.maximum(row_max, jnp.max(score, 0, keepdims=True))
    total = jnp.zeros((1, two), jnp.float32)
    weighted = jnp.zeros((1, two), jnp.float32)
    for piece, place in enumerate(places):
        raised = jnp.exp2((score_ref[piece] - row_max) * (scale * LOG2E))
        dprob = jnp.dot(value_low[place], do_turned, preferred_element_type=jnp.float32)
        score_ref[piece] = raised
        dprob_ref[piece] = dprob
        total = total + jnp.sum(raised, 0, keepdims=True)
        weighted = weighted + jnp.sum(raised * dprob, 0, keepdims=True)
    inverse = 1.0 / total
    delta = weighted * inverse
    attended = jnp.zeros((HEAD_DIM, two), jnp.float32)
    grad_q = jnp.zeros((HEAD_DIM, two), jnp.float32)
    for piece in range(0, len(places), 2):
        lows, dlows = [], []
        for step in (piece, piece + 1):
            rows = pl.ds(pl.multiple_of(places[step] * BLOCK, BLOCK), BLOCK)
            probs = score_ref[step] * inverse
            probs_low = probs.astype(jnp.bfloat16)
            dscore = (probs * (dprob_ref[step] - delta)).astype(jnp.bfloat16)
            value_grad[rows] += jnp.dot(probs_low, do_rows, preferred_element_type=jnp.float32)
            key_grad[rows] += jnp.dot(dscore, q_rows, preferred_element_type=jnp.float32)
            lows.append(probs_low)
            dlows.append(dscore)
        here, there = places[piece], places[piece + 1]
        value_two = jnp.concatenate([value_turned[here], value_turned[there]], 1)
        key_two = jnp.concatenate([key_turned[here], key_turned[there]], 1)
        attended = attended + jnp.dot(
            value_two, jnp.concatenate(lows, 0), preferred_element_type=jnp.float32
        )
        grad_q = grad_q + jnp.dot(
            key_two, jnp.concatenate(dlows, 0), preferred_element_type=jnp.float32
        )
    return attended.T.astype(jnp.bfloat16), (grad_q * scale).T.astype(jnp.bfloat16)


def coarsen_gradients(weight, bases, blocks, levels, wide_ref, grad_ref, put_weight_grad):
    for level_id in range(levels, 0, -1):
        tap_sums = [jnp.zeros((1, HEAD_DIM), jnp.float32) for _ in range(4)]
        for block in range(blocks >> level_id):
            start = (bases[level_id] + 1 + block) * BLOCK
            upstream = grad_ref[start : start + BLOCK]
            following = grad_ref[start + 1 : start + 1 + BLOCK]
            below = (bases[level_id - 1] + 1 + 2 * block) * BLOCK
            taps = [weight(4 * (level_id - 1) + tap) for tap in range(4)]
            grad_ref[pl.ds(below, BLOCK, stride=2)] += taps[2] * upstream + taps[0] * following
            grad_ref[pl.ds(below + 1, BLOCK, stride=2)] += taps[3] * upstream + taps[1] * following
            for tap in range(4):
                tap_sums[tap] = tap_sums[tap] + jnp.sum(
                    upstream * wide_ref[pl.ds(below - 2 + tap, BLOCK, stride=2)], 0, keepdims=True
                )
        for tap in range(4):
            put_weight_grad(4 * (level_id - 1) + tap, tap_sums[tap])


def columns(head):
    return pl.ds(pl.multiple_of(head * HEAD_DIM, HEAD_DIM), HEAD_DIM)


def head_kernel(
    levels,
    ring,
    groups,
    q_hbm,
    key_hbm,
    value_hbm,
    do_hbm,
    conv_key_ref,
    conv_value_ref,
    att_hbm,
    grad_q_hbm,
    grad_key_hbm,
    grad_value_hbm,
    conv_key_grad,
    conv_value_grad,
    rows_ref,
    out_ref,
    conv_here,
    conv_parts,
    conv_slots,
    edge_ref,
    halo_out,
    halo_in,
    chain_out,
    chain_in,
    key_wide,
    key_low,
    key_turned,
    key_grad,
    value_wide,
    value_low,
    value_turned,
    value_grad,
    score_ref,
    dprob_ref,
    in_send,
    in_recv,
    out_send,
    out_recv,
    edge_send,
    edge_recv,
    block_send,
    block_recv,
    halo_send,
    halo_recv,
    chain_send,
    chain_recv,
    part_send,
    part_recv,
    total_send,
    total_recv,
):
    me = lax.axis_index("seq")
    group = lax.axis_index("dp")
    size = ring // 2
    heads = HEADS // size
    half = me // size
    rank = lax.rem(me, size)
    partner = lax.rem(me + size, ring)
    blocks = 2 * size
    bases, _ = level_bases(blocks, levels)
    scale = HEAD_DIM**-0.5
    sources = (q_hbm, key_hbm, value_hbm, do_hbm)
    conv_grads = (conv_key_grad, conv_value_grad)
    results = (att_hbm, grad_q_hbm, grad_key_hbm, grad_value_hbm)
    lows = (key_low, value_low)
    turned = (key_turned, value_turned)
    grads = (key_grad, value_grad)
    wides = (key_wide, value_wide)

    def after(distance):
        return lax.rem(rank + distance, size)

    def before(distance):
        return lax.rem(rank + size - distance, size)

    barrier = pltpu.get_barrier_semaphore()
    for distance in range(1, ring):
        pl.semaphore_signal(
            barrier,
            inc=1,
            device_id={"seq": lax.rem(me + distance, ring)},
            device_id_type=pl.DeviceIdType.MESH,
        )
    for distance in range(1, groups):
        pl.semaphore_signal(
            barrier,
            inc=1,
            device_id={"dp": lax.rem(group + distance, groups)},
            device_id_type=pl.DeviceIdType.MESH,
        )
    pl.semaphore_wait(barrier, ring + groups - 2)

    def to_seq(source, target, send_sem, recv_sem, device):
        return pltpu.make_async_remote_copy(
            src_ref=source,
            dst_ref=target,
            send_sem=send_sem,
            recv_sem=recv_sem,
            device_id={"seq": device},
            device_id_type=pl.DeviceIdType.MESH,
        )

    def inbound(array, distance, head, landing):
        place = (array, distance, head)
        return to_seq(
            sources[array].at[0, :, columns(after(distance) * heads + head)],
            rows_ref.at[landing, array, head],
            in_send.at[place],
            in_recv.at[place],
            half * size + after(distance),
        )

    def inbound_own(array, head):
        return pltpu.make_async_copy(
            sources[array].at[0, :, columns(rank * heads + head)],
            rows_ref.at[rank, array, head],
            in_recv.at[array, 0, head],
        )

    def outbound(array, distance, head, origin):
        place = (array, distance, head)
        return to_seq(
            out_ref.at[before(distance), array, head],
            results[array].at[0, :, columns(origin * heads + head)],
            out_send.at[place],
            out_recv.at[place],
            half * size + before(distance),
        )

    def outbound_own(array, head):
        return pltpu.make_async_copy(
            out_ref.at[rank, array, head],
            results[array].at[0, :, columns(rank * heads + head)],
            out_recv.at[array, 0, head],
        )

    def edge_copy(kind, head, other):
        return to_seq(
            sources[1 + kind].at[0, pl.ds(2 * BLOCK - EDGE, EDGE), columns(other * heads + head)],
            edge_ref.at[kind, head],
            edge_send.at[kind, head, other],
            edge_recv.at[kind, head],
            size + other,
        )

    def edge_place(level_id):
        count = blocks >> level_id
        return bases[level_id] + count - half * (count - 1)

    def pad_place(level_id, of_half):
        return bases[level_id] + (1 - of_half) * ((blocks >> level_id) + 1)

    def block_copy(kind, level_id, head, pad):
        place = (kind, level_id, head)
        return to_seq(
            lows[kind].at[head, edge_place(level_id)],
            lows[kind].at[head, pad],
            block_send.at[place],
            block_recv.at[place],
            partner,
        )

    def halo_copy(kind, level_id, head):
        place = (kind, level_id, head)
        return to_seq(
            halo_out.at[place], halo_in.at[place], halo_send.at[place], halo_recv.at[place], partner
        )

    def chain_copy(kind, head):
        return to_seq(
            chain_out.at[kind, head],
            chain_in.at[kind, head],
            chain_send.at[kind, head],
            chain_recv.at[kind, head],
            partner,
        )

    every = [(kind, head) for head in range(heads) for kind in range(2)]

    @pl.when(me == size - 1)
    def _():
        for kind, head in every:
            for other in range(size):
                edge_copy(kind, head, other).start()

    @pl.when(half == 0)
    def _():
        edge_ref[...] = jnp.zeros_like(edge_ref)

    def send(head, *arrays):
        for array in arrays:
            inbound_own(array, head).start()

        def step(distance, carry):
            for array in arrays:
                inbound(array, distance, head, rank).start()
            return carry

        lax.fori_loop(1, size, step, 0)

    for head in range(heads):
        send(head, 1)
        send(head, 2)
        send(head, 0, 3)
    for head in range(heads):
        conv_here[0, head] = conv_key_ref[:, :, columns(rank * heads + head)]
        conv_here[1, head] = conv_value_ref[:, :, columns(rank * heads + head)]

    def arrived(array, distance, head):
        @pl.when(distance == 0)
        def _():
            inbound_own(array, head).wait()

        @pl.when(distance > 0)
        def _():
            inbound(array, distance, head, before(distance)).wait_recv()

    def leave(array, distance, head):
        @pl.when(distance == 0)
        def _():
            outbound_own(array, head).start()

        @pl.when(distance > 0)
        def _():
            outbound(array, distance, head, rank).start()

    def taker(array, head):
        def take_rows(distance):
            arrived(array, distance, head)
            return before(distance), rows_ref[before(distance), array, head]

        return take_rows

    def weight_of(kind, head):
        def weight(row):
            return conv_here[kind, head, row // 4, row % 4 : row % 4 + 1]

        return weight

    shape = (bases, blocks, levels)
    key_grad[...] = jnp.zeros_like(key_grad)
    value_grad[...] = jnp.zeros_like(value_grad)

    @pl.when(half == 1)
    def _():
        for kind, head in every:
            edge_copy(kind, head, rank).wait_recv()

    for kind, head in every:
        build_levels(
            taker(1 + kind, head),
            edge_ref[kind, head],
            half,
            weight_of(kind, head),
            *shape,
            wides[kind].at[head],
            lows[kind].at[head],
            turned[kind].at[head],
        )
        for level_id in range(levels, -1, -1):
            block_copy(kind, level_id, head, pad_place(level_id, 1 - half)).start()

    def step(index, carry):
        head = index // size
        count = lax.rem(index, size)

        @pl.when(count == 0)
        def _():
            for kind in range(2):
                for level_id in range(levels, -1, -1):
                    pad = pad_place(level_id, half)
                    block_copy(kind, level_id, head, pad).wait_recv()
                    wide = lows[kind][head, pad].astype(jnp.float32)
                    turned[kind][head, pad] = wide.T.astype(jnp.bfloat16)

        pair = (1 - half) * (size - 1 - count) + half * count
        distance = lax.rem(rank + size - pair, size)
        arrived(0, distance, head)
        arrived(3, distance, head)
        attended, grad_q = attend_pair(
            pair,
            half * size + pair,
            ring,
            rows_ref[pair, 0, head],
            rows_ref[pair, 3, head],
            *shape,
            (key_low.at[head], key_turned.at[head], key_grad.at[head]),
            (value_low.at[head], value_turned.at[head], value_grad.at[head]),
            (score_ref, dprob_ref),
        )
        out_ref[pair, 0, head] = attended
        out_ref[pair, 1, head] = grad_q
        leave(0, distance, head)
        leave(1, distance, head)
        for level_id in range(levels + 1):

            @pl.when(count == max(1, 1 << level_id >> 1) - 1)
            def _(level_id=level_id):
                start = pl.multiple_of(pad_place(level_id, half) * BLOCK, BLOCK)
                for kind in range(2):
                    rows = grads[kind][head, pl.ds(start, BLOCK)]
                    halo_out[kind, level_id, head] = rows.astype(jnp.bfloat16)
                    halo_copy(kind, level_id, head).start()

        return carry

    lax.fori_loop(0, size * heads, step, 0)

    def finisher(array, head, grad_ref, factor):
        def finish(distance, carry):
            pair = before(distance)
            rows = pl.ds(pl.multiple_of((1 + 2 * pair) * BLOCK, BLOCK), 2 * BLOCK)
            out_ref[pair, array, head] = (grad_ref[head, rows] * factor).astype(jnp.bfloat16)
            leave(array, distance, head)
            return carry

        return finish

    for kind, head in every:
        grad_ref = grads[kind].at[head]
        for level_id in range(levels + 1):
            halo_copy(kind, level_id, head).wait_recv()
            rows = pl.ds(pl.multiple_of(edge_place(level_id) * BLOCK, BLOCK), BLOCK)
            grad_ref[rows] += halo_in[kind, level_id, head].astype(jnp.float32)

        @pl.when(half == 0)
        def _(kind=kind, head=head, grad_ref=grad_ref):
            chain_copy(kind, head).wait_recv()
            for level_id in range(1, levels + 1):
                start = (bases[level_id] + (blocks >> level_id) + 1) * BLOCK
                grad_ref[start : start + 8] = chain_in[kind, head, level_id - 1]

        def put(row, value, kind=kind, head=head):
            factor = 1.0 if kind else scale
            here = slice(head * HEAD_DIM, (head + 1) * HEAD_DIM)
            conv_parts[group, kind, row // 4, row % 4 : row % 4 + 1, here] = value * factor

        coarsen_gradients(weight_of(kind, head), *shape, wides[kind].at[head], grad_ref, put)

        @pl.when(half == 1)
        def _(kind=kind, head=head, grad_ref=grad_ref):
            for level_id in range(1, levels + 1):
                start = (bases[level_id] + 1) * BLOCK
                chain_out[kind, head, level_id - 1] = grad_ref[start : start + 8]
            chain_copy(kind, head).start()

        lax.fori_loop(0, size, finisher(2 + kind, head, grads[kind], 1.0 if kind else scale), 0)

    def part(distance, slot):
        return pltpu.make_async_remote_copy(
            src_ref=conv_parts.at[group],
            dst_ref=conv_parts.at[slot],
            send_sem=part_send.at[distance],
            recv_sem=part_recv.at[distance],
            device_id={"dp": lax.rem(group + distance, groups)},
            device_id_type=pl.DeviceIdType.MESH,
        )

    def gathered(distance, slot):
        return to_seq(
            conv_slots.at[me],
            conv_slots.at[slot],
            total_send.at[distance],
            total_recv.at[distance],
            lax.rem(me + distance, ring),
        )

    for distance in range(1, groups):
        part(distance, group).start()
    for distance in range(1, groups):
        part(distance, lax.rem(group + groups - distance, groups)).wait_recv()
    conv_sum = conv_parts[0]
    for slot in range(1, groups):
        conv_sum = conv_sum + conv_parts[slot]
    conv_slots[me] = conv_sum
    for distance in range(1, ring):
        gathered(distance, me).start()
    for distance in range(1, ring):
        gathered(distance, lax.rem(me + ring - distance, ring)).wait_recv()
    width = heads * HEAD_DIM
    for kind in range(2):
        for slot in range(size):
            both = conv_slots[slot, kind] + conv_slots[size + slot, kind]
            conv_grads[kind][:, :, slot * width : (slot + 1) * width] = both

    for array in range(4):
        for head in range(heads):
            outbound_own(array, head).wait()

    def settle(distance, carry):
        for array in range(4):
            for head in range(heads):
                inbound(array, distance, head, rank).wait_send()
                outbound(array, distance, head, rank).wait_send()
                outbound(array, distance, head, after(distance)).wait_recv()
        return carry

    lax.fori_loop(1, size, settle, 0)
    for distance in range(1, ring):
        gathered(distance, me).wait_send()
    for distance in range(1, groups):
        part(distance, group).wait_send()
    for kind, head in every:
        for level_id in range(levels + 1):
            block_copy(kind, level_id, head, pad_place(level_id, 1 - half)).wait_send()
            halo_copy(kind, level_id, head).wait_send()

    @pl.when(half == 1)
    def _():
        for kind, head in every:
            chain_copy(kind, head).wait_send()

    @pl.when(me == size - 1)
    def _():
        for kind, head in every:
            for other in range(size):
                edge_copy(kind, head, other).wait_send()


def stack_scratch(heads, blocks, levels):
    total = level_bases(blocks, levels)[1]
    flat = pltpu.VMEM((heads, total * BLOCK, HEAD_DIM), jnp.float32)
    low = pltpu.VMEM((heads, total, BLOCK, HEAD_DIM), jnp.bfloat16)
    return [flat, low, low, flat]


def per_device_heads(queries, key_rows, value_rows, conv_key, conv_value, grad_out):
    tok_rows = queries.shape[1]
    levels = conv_key.shape[0]
    ring, groups = lax.axis_size("seq"), lax.axis_size("dp")
    size = ring // 2
    heads = HEADS // size
    like = jax.ShapeDtypeStruct(queries.shape, jnp.bfloat16)
    conv_like = jax.ShapeDtypeStruct(conv_key.shape, jnp.float32)
    scores = pltpu.VMEM((4 + 2 * levels, BLOCK, 2 * BLOCK), jnp.float32)
    rows = pltpu.VMEM((size, 4, heads, tok_rows, HEAD_DIM), jnp.bfloat16)
    conv_part = (2, levels, 4, heads * HEAD_DIM)
    halo = pltpu.VMEM((2, levels + 1, heads, BLOCK, HEAD_DIM), jnp.bfloat16)
    chain = pltpu.VMEM((2, heads, levels, 8, HEAD_DIM), jnp.float32)
    dma = pltpu.SemaphoreType.DMA
    in_hbm = pl.BlockSpec(memory_space=pltpu.HBM)
    anywhere = pl.BlockSpec(memory_space=pl.ANY)
    in_vmem = pl.BlockSpec(memory_space=pltpu.VMEM)
    return pl.pallas_call(
        functools.partial(head_kernel, levels, ring, groups),
        out_shape=(like, like, like, like, conv_like, conv_like),
        in_specs=[in_hbm] * 4 + [in_vmem] * 2,
        out_specs=[anywhere] * 4 + [in_vmem] * 2,
        scratch_shapes=[
            rows,
            rows,
            pltpu.VMEM((2, heads, levels, 4, HEAD_DIM), jnp.float32),
            pltpu.VMEM((groups,) + conv_part, jnp.float32),
            pltpu.VMEM((ring,) + conv_part, jnp.float32),
            pltpu.VMEM((2, heads, EDGE, HEAD_DIM), jnp.bfloat16),
            halo,
            halo,
            chain,
            chain,
        ]
        + stack_scratch(heads, 2 * size, levels) * 2
        + [scores, scores]
        + [dma((4, size, heads))] * 4
        + [dma((2, heads, size)), dma((2, heads))]
        + [dma((2, levels + 1, heads))] * 4
        + [dma((2, heads))] * 2
        + [dma((groups,))] * 2
        + [dma((ring,))] * 2,
        compiler_params=pltpu.CompilerParams(
            collective_id=0, has_side_effects=True, vmem_limit_bytes=56 * 2**20
        ),
    )(queries, key_rows, value_rows, grad_out, conv_key, conv_value)


def solution(mesh):
    in_specs = (
        P("dp", "seq", None),
        P("dp", "seq", None),
        P("dp", "seq", None),
        P(),
        P(),
        P("dp", "seq", None),
    )
    out_specs = (
        P("dp", "seq", None),
        P("dp", "seq", None),
        P("dp", "seq", None),
        P("dp", "seq", None),
        P(),
        P(),
    )
    def chosen(*args):
        seq_devices = lax.axis_size("seq")
        fits = seq_devices == HEADS and args[0].shape[:2] == (1, 2 * BLOCK)
        fits = fits and seq_devices >> args[3].shape[0] >= 1
        return (per_device_heads if fits else per_device)(*args)

    return jax.shard_map(
        chosen, mesh=mesh, in_specs=in_specs, out_specs=out_specs, check_vma=False
    )
```
